32 devices in a mesh: group: 2 (over y), head: 8 (over z, x), dp: 2 (over core).
Axes of the slice: x: 2, y: 2, z: 4, core: 2. Of those that a mesh axis runs over, the one named last changes fastest.
Arguments:
- queries: bfloat16 [32, 16384], P(('group', 'dp'), 'head'), parts along dimension 0, may hold values from -6 to 6
- new_kv: bfloat16 [32, 2, 1024], P(('group', 'dp')), parts along dimension 0, may hold values from -6 to 6
- positions: int32 [32], P(('group', 'dp')), parts along dimension 0, may hold values from 256 to 1023
- lengths: int32 [32], P(('group', 'dp')), parts along dimension 0, may hold values from 2 to 256, as said below
- kv_codes: bfloat16 [32, 2, 256, 1024], P(('group', 'dp'), None, 'head'), parts along dimension 0, may hold values from -8 to 7, as said below
- kv_scales: float32 [32, 2, 8, 256], P(('group', 'dp'), None, None, 'head'), parts along dimension 0, may hold values from 0.1 to 40
- wo_codes: bfloat16 [16384, 16384], P('head'), may hold values from -8 to 7, as said below
- wo_scales: float32 [16384], P('head'), may hold values from 0.004 to 0.03
- residual: bfloat16 [32, 16384], P(('group', 'dp'), 'head'), parts along dimension 0, may hold values from -6 to 6
Outputs:
- hidden_out: bfloat16 [32, 16384], P(('group', 'dp'), 'head'), parts along dimension 0
The draws below stay inside these ranges and needn't reach their ends.
There are 2 independent parts, one for each index of `group`. The reference program is written for one: setup_inputs(seed, part) draws one part's arguments, and reference() takes and returns one part's arrays. A program takes and returns all parts, laid end to end along the dimension named above; an argument that names none is the same for every part. Nothing has to cross between parts.
Inputs may be any that keep to these rules, and one draw needn't show every extreme that they name: Each row has at least two live slots, which are slots 0 to lengths - 1 of every key-value head; some row is full (256 live slots). `kv_codes`: integer codes. `wo_codes`: integer codes.
All inputs are finite; a program needn't handle non-finite values.
Results may differ from the reference program's by a relative error of at most 0.0089.
Values may be sent and summed in bfloat16 or wider, within the bound.
A program may use at most 128 MiB of HBM per device.

```python
import math
import jax
import jax.numpy as jnp
from jax import lax

D = 16384
H = 128
KVH = 8
HD = 128
CTX = 256
ROWS = 16


def draw_lengths(key, part):
    key_base, key_extra = jax.random.split(jax.random.fold_in(key, 11))
    drawn = jax.random.randint(key_base, (ROWS,), 2, CTX + 1)
    full_row = jax.random.randint(key_extra, (), 0, ROWS)
    return jnp.where(jnp.arange(ROWS) == full_row, CTX, drawn).astype(jnp.int32)


def draw_kv_codes(key, part):
    drawn = jax.random.randint(jax.random.fold_in(key, 3), (ROWS, 2, CTX, KVH, HD), -8, 8).astype(jnp.float32)
    return drawn.reshape(ROWS, 2, CTX, KVH * HD).astype(jnp.bfloat16)


def draw_kv_scales(key, part):
    key_base = jax.random.fold_in(jax.random.fold_in(key, 5), 0)
    drawn = jnp.exp(jax.random.uniform(key_base, (ROWS, 2, KVH, CTX), minval=math.log(0.1), maxval=math.log(0.3)))
    return drawn.astype(jnp.float32)


def draw_wo_codes(key, part):
    drawn = jax.random.randint(jax.random.fold_in(key, 7), (H * HD, D), -8, 8).astype(jnp.float32)
    return drawn.astype(jnp.bfloat16)


def place_ends(result, stream_key, low, top_value):
    longest = result.shape.index(max(result.shape))
    spots = []
    for shift in (0, 1):
        where = [jax.random.randint(jax.random.fold_in(stream_key, axis), (), 0, length) for axis, length in enumerate(result.shape)]
        where[longest] = (where[longest] + shift) % result.shape[longest]
        spots.append(tuple(where))
    return result.at[spots[0]].set(low).at[spots[1]].set(top_value)


def block_scale(key, shape, pieces, smallest, high):
    loudness = 1.0
    for dim, parts in pieces:
        draws = jax.random.uniform(jax.random.fold_in(jax.random.fold_in(key, 6), dim), (parts,), jnp.float32, smallest / len(pieces), high / len(pieces))
        loudness = loudness * jnp.repeat(jnp.exp(draws), shape[dim] // parts).reshape((-1,) + (1,) * (len(shape) - 1 - dim))
    return loudness


def bell_draw(own_key, extent, deviation, bound, cuts=(), kind=jnp.bfloat16):
    values = deviation * jax.random.normal(own_key, extent, jnp.float32)
    if cuts:
        values = values * block_scale(own_key, extent, cuts, -0.22, 0.18)
    return jnp.clip(values, -bound, bound).astype(kind)


def setup_inputs(seed: int = 0, part: int = 0) -> dict:
    key_of = jax.random.split(jax.random.key(seed), 10)
    part_keys = jax.random.split(jax.random.fold_in(key_of[9], part), 10)
    queries = bell_draw(part_keys[0], (ROWS, H * HD), 1.0, 6.0, ((0, 2), (1, 8)))
    new_kv = bell_draw(part_keys[1], (ROWS, 2, KVH * HD), 1.0, 6.0, ((0, 2),))
    positions = place_ends(jax.random.randint(part_keys[2], (ROWS,), CTX, 4 * CTX), jax.random.fold_in(part_keys[2], 1), CTX, (4 * CTX) - 1).astype(jnp.int32)
    lengths = draw_lengths(jax.random.fold_in(jax.random.fold_in(key_of[9], part), 71), part)
    kv_codes = draw_kv_codes(jax.random.fold_in(jax.random.fold_in(key_of[9], part), 71), part)
    kv_scales = draw_kv_scales(jax.random.fold_in(jax.random.fold_in(key_of[9], part), 71), part)
    wo_codes = draw_wo_codes(jax.random.fold_in(key_of[9], 71), part)
    wo_scales = jnp.clip(jnp.exp(math.log(0.03) - 2.014903 * jax.random.uniform(key_of[7], (D,), jnp.float32) ** block_scale(key_of[7], (D,), ((0, 8),), -0.2, 0.2)), 0.004, 0.03)
    residual = bell_draw(part_keys[8], (ROWS, D), 1.0, 6.0, ((0, 2), (1, 8)))
    return {"queries": queries, "new_kv": new_kv, "positions": positions, "lengths": lengths, "kv_codes": kv_codes, "kv_scales": kv_scales, "wo_codes": wo_codes, "wo_scales": wo_scales, "residual": residual}


ROPE_BASE = 500000.0
NEG_FILL = -1.0e30


def rotary(values_in, positions):
    half_dim = values_in.shape[-1] // 2
    inverse_rate = ROPE_BASE ** (-(jnp.arange(half_dim, dtype=jnp.float32) * (2.0 / values_in.shape[-1])))
    angles = positions.astype(jnp.float32)[:, None, None] * inverse_rate
    cosine = jnp.cos(angles)
    sine_part = jnp.sin(angles)
    lower_half = values_in[..., :half_dim]
    upper_half = values_in[..., half_dim:]
    return jnp.concatenate([lower_half * cosine - upper_half * sine_part, upper_half * cosine + lower_half * sine_part], axis=-1)


def hadamard(size_needed):
    index_row = jnp.arange(size_needed, dtype=jnp.int32)
    common = jnp.bitwise_and(index_row[:, None], index_row[None, :])
    parity = jnp.zeros_like(common)
    for bit_pos in range(max(size_needed.bit_length() - 1, 0)):
        parity = parity + jnp.right_shift(common, bit_pos) % 2
    return jnp.where(parity % 2 == 0, 1.0, -1.0).astype(jnp.float32)


def reference(queries, new_kv, positions, lengths, kv_codes, kv_scales, wo_codes, wo_scales, residual):
    n_rows = queries.shape[0]
    group_size = H // KVH
    score_scale = HD ** -0.5
    query_rot = rotary(queries.reshape(n_rows, H, HD).astype(jnp.float32), positions).astype(jnp.bfloat16)
    fresh_keys = rotary(new_kv[:, 0].reshape(n_rows, KVH, HD).astype(jnp.float32), positions).astype(jnp.bfloat16)
    fresh_values = new_kv[:, 1].reshape(n_rows, KVH, HD).astype(jnp.float32)
    query_groups = query_rot.reshape(n_rows, KVH, group_size, HD).astype(jnp.float32)
    cache_codes = kv_codes.reshape(n_rows, 2, CTX, KVH, HD).astype(jnp.float32)
    cache_scales = kv_scales
    raw_scores = jnp.einsum("rgjd,rtgd->rgjt", query_groups, cache_codes[:, 0], precision=lax.Precision.HIGHEST)
    scores = raw_scores * cache_scales[:, 0][:, :, None, :] * score_scale
    is_valid = (jnp.arange(CTX, dtype=jnp.int32)[None, :] < lengths[:, None])[:, None, None, :]
    scores = jnp.where(is_valid, scores, NEG_FILL)
    fresh_score = jnp.einsum("rgjd,rgd->rgj", query_groups, fresh_keys.astype(jnp.float32), precision=lax.Precision.HIGHEST) * score_scale
    peak_all = jnp.maximum(jnp.max(scores, axis=-1), fresh_score)
    weights = jnp.where(is_valid, jnp.exp(scores - peak_all[..., None]), 0.0)
    fresh_weight = jnp.exp(fresh_score - peak_all)
    total_all = jnp.sum(weights, axis=-1) + fresh_weight
    weighted = jnp.einsum("rgjt,rtgd->rgjd", weights * cache_scales[:, 1][:, :, None, :], cache_codes[:, 1], precision=lax.Precision.HIGHEST)
    weighted = weighted + fresh_weight[..., None] * fresh_values[:, :, None, :]
    attended = (weighted / total_all[..., None]).reshape(n_rows, H, HD).astype(jnp.bfloat16)
    sylvester = hadamard(H)
    rotated = jnp.einsum("ij,rjd->rid", sylvester, attended.astype(jnp.float32), precision=lax.Precision.HIGHEST) * (H ** -0.5)
    flat_rows = rotated.reshape(n_rows, H * HD).astype(jnp.bfloat16)
    projected = jnp.dot(flat_rows, wo_codes, preferred_element_type=jnp.float32) * wo_scales
    return (residual.astype(jnp.float32) + projected).astype(jnp.bfloat16)
```

```python
import functools
import math

import jax
import jax.numpy as jnp
from jax import lax
from jax.experimental import pallas as pl
from jax.experimental.pallas import tpu as pltpu
from jax.sharding import PartitionSpec as P

H = 128
KVH = 8
HD = 128


ROPE_BASE = 500000.0
NEG_FILL = -1e30


def partner_2(block, axis, distance):
    count = lax.axis_size(axis)
    route = []
    for low in range(count):
        high = low | 1 << distance
        if high != low and high < count:
            route += [(low, high), (high, low)]
    return lax.ppermute(block, axis, route)


def rotary(values_in, positions):
    half_dim = values_in.shape[-1] // 2
    inverse_rate = ROPE_BASE ** (
        -(jnp.arange(half_dim, dtype=jnp.float32) * (2.0 / values_in.shape[-1]))
    )
    angles = positions.astype(jnp.float32)[:, None, None] * inverse_rate
    cosine = jnp.cos(angles)
    sine_part = jnp.sin(angles)
    lower_half = values_in[..., :half_dim]
    upper_half = values_in[..., half_dim:]
    return jnp.concatenate(
        [
            lower_half * cosine - upper_half * sine_part,
            upper_half * cosine + lower_half * sine_part,
        ],
        axis=-1,
    )


def hadamard(size_needed):
    index_row = jnp.arange(size_needed, dtype=jnp.int32)
    common = jnp.bitwise_and(index_row[:, None], index_row[None, :])
    parity = jnp.zeros_like(common)
    for bit_pos in range(max(size_needed.bit_length() - 1, 0)):
        parity = parity + jnp.right_shift(common, bit_pos) % 2
    return jnp.where(parity % 2 == 0, 1.0, -1.0).astype(jnp.float32)


def settle(peak_source, total_source, summed_source, fresh_score, fresh_values):
    peak_final = jnp.maximum(jnp.max(peak_source, axis=1), fresh_score)
    rescale = jnp.exp(peak_source - peak_final[:, None])
    fresh_weight = jnp.exp(fresh_score - peak_final)
    total_final = jnp.sum(total_source * rescale, axis=1) + fresh_weight
    summed_final = (
        jnp.sum(summed_source * rescale[..., None], axis=1) + fresh_weight[..., None] * fresh_values
    )
    return (summed_final / total_final[..., None]).astype(jnp.bfloat16)


def on_device_general(
    queries, new_kv, positions, lengths, kv_codes, kv_scales, wo_codes, wo_scales, residual
):
    n_head = lax.axis_size("head")
    my_index = lax.axis_index("head")
    n_rows = queries.shape[0]
    heads_here = queries.shape[1] // HD
    group_size = H // KVH
    block_len = kv_codes.shape[2]
    first_slot = my_index * block_len
    score_scale = HD ** (-0.5)
    own_query = rotary(
        queries.reshape(n_rows, heads_here, HD).astype(jnp.float32), positions
    ).astype(jnp.bfloat16)
    all_query = lax.all_gather(
        own_query.reshape(n_rows, heads_here * HD), "head", axis=1, tiled=True
    )
    all_query = all_query.reshape(n_rows, KVH, group_size, HD)
    fresh_keys = rotary(
        new_kv[:, 0].reshape(n_rows, KVH, HD).astype(jnp.float32), positions
    ).astype(jnp.bfloat16)
    fresh_values = new_kv[:, 1].reshape(n_rows, KVH, HD).astype(jnp.float32)
    key_codes = kv_codes[:, 0].reshape(n_rows, block_len, KVH, HD)
    value_codes = kv_codes[:, 1].reshape(n_rows, block_len, KVH, HD).astype(jnp.float32)
    raw_scores = jnp.einsum(
        "rgjd,rtgd->rgjt", all_query, key_codes, preferred_element_type=jnp.float32
    )
    scores = raw_scores * kv_scales[:, 0][:, :, None, :] * score_scale
    slot_index = first_slot + jnp.arange(block_len, dtype=jnp.int32)
    is_valid = (slot_index[None, :] < lengths[:, None])[:, None, None, :]
    scores = jnp.where(is_valid, scores, NEG_FILL)
    peak_here = jnp.max(scores, axis=-1)
    weights = jnp.where(is_valid, jnp.exp(scores - peak_here[..., None]), 0.0)
    total_here = jnp.sum(weights, axis=-1)
    summed = jnp.einsum(
        "rgjt,rtgd->rgjd",
        weights * kv_scales[:, 1][:, :, None, :],
        value_codes,
        precision=lax.Precision.HIGHEST,
    )
    peak_full = peak_here.reshape(n_rows, H)
    total_full = total_here.reshape(n_rows, H)
    summed_full = summed.reshape(n_rows, H, HD)
    received = (
        lax.all_to_all(peak_full, "head", split_axis=1, concat_axis=1, tiled=True),
        lax.all_to_all(total_full, "head", split_axis=1, concat_axis=1, tiled=True),
        lax.all_to_all(summed_full, "head", split_axis=1, concat_axis=1, tiled=True),
    )
    peak_source = received[0].reshape(n_rows, n_head, heads_here)
    total_source = received[1].reshape(n_rows, n_head, heads_here)
    summed_source = received[2].reshape(n_rows, n_head, heads_here, HD)
    owned_group = my_index * heads_here // group_size
    key_owned = lax.dynamic_index_in_dim(fresh_keys, owned_group, 1, keepdims=False)
    fresh_score = (
        jnp.einsum("rjd,rd->rj", own_query, key_owned, preferred_element_type=jnp.float32)
        * score_scale
    )
    value_owned = lax.dynamic_index_in_dim(fresh_values, owned_group, 1, keepdims=False)
    fresh_spread = jnp.broadcast_to(value_owned[:, None, :], (n_rows, heads_here, HD))
    attended = settle(peak_source, total_source, summed_source, fresh_score, fresh_spread)
    local_table = hadamard(heads_here)
    rotated = jnp.einsum(
        "kj,rjd->rkd", local_table, attended.astype(jnp.float32), precision=lax.Precision.HIGHEST
    )
    for bit_pos in range(n_head.bit_length() - 1):
        partner = partner_2(rotated, "head", bit_pos)
        is_upper = jnp.right_shift(my_index, bit_pos) % 2 == 1
        rotated = jnp.where(is_upper, partner - rotated, rotated + partner)
    flat_rows = (rotated * H ** (-0.5)).reshape(n_rows, heads_here * HD).astype(jnp.bfloat16)
    partial_out = jnp.dot(flat_rows, wo_codes, preferred_element_type=jnp.float32)
    shares = lax.psum_scatter(partial_out, "head", scatter_dimension=1, tiled=True)
    return (residual.astype(jnp.float32) + shares * wo_scales).astype(jnp.bfloat16)


PEAK_FLOOR = -1e29
DEVICE = pl.DeviceIdType.MESH


def fused_kernel(
    n,
    positions,
    lengths,
    queries,
    new_kv,
    rates,
    residual,
    wo_scales,
    kv_scales,
    kv_codes,
    wo_codes,
    out,
    q_all,
    kv_here,
    scale_lanes,
    part_out,
    part_in,
    stat_out,
    stat_in,
    rot_out,
    rot_in,
    wo_here,
    share_out,
    share_in,
    kv_sem,
    wo_sem,
    q_send,
    q_recv,
    part_send,
    part_recv,
    stat_send,
    stat_recv,
    rot_send,
    rot_recv,
    share_send,
    share_recv,
):
    me = lax.axis_index("head")
    core = lax.axis_index("dp")
    n_rows = queries.shape[0]
    group = queries.shape[1] // HD
    block_len = kv_codes.shape[2]
    wide = wo_here.shape[2]
    half_wide = wide // 2
    halves = n_rows * block_len // HD
    rows_half = n_rows // halves
    score_scale = HD ** (-0.5)
    f32 = jnp.float32

    def peer_of(step):
        return lax.rem(me + step, n)

    def to(head, dp):
        return {"head": head, "dp": dp}

    kv_copy = pltpu.make_async_copy(kv_codes, kv_here, kv_sem)
    kv_copy.start()

    def wo_copy(i):
        first = pl.multiple_of(i * (2 * wide) + core * wide, wide)
        return pltpu.make_async_copy(
            wo_codes.at[:, pl.ds(first, wide)], wo_here.at[i], wo_sem.at[i]
        )

    for step in range(1, n + 1):
        wo_copy(peer_of(step)).start()

    barrier = pltpu.get_barrier_semaphore()
    for step in range(n):
        for other in range(2):
            if step or other:
                pl.semaphore_signal(
                    barrier,
                    inc=1,
                    device_id=to(peer_of(step), lax.rem(core + other, 2)),
                    device_id_type=DEVICE,
                )

    lane_1 = lax.broadcasted_iota(jnp.int32, (1, HD), 1)
    row_8 = lax.broadcasted_iota(jnp.int32, (n_rows, HD), 0)
    pos = jnp.zeros((n_rows, HD), f32)
    for r in range(n_rows):
        pos = jnp.where(row_8 == r, positions[r].astype(f32), pos)
    sign = jnp.where(lane_1 < HD // 2, -1.0, 1.0).astype(f32)
    angle = pos * rates[...]
    cosine = jnp.cos(angle)
    sine = jnp.sin(angle) * sign

    def turn(v, c, s):
        return v * c + pltpu.roll(v, HD // 2, 1) * s

    stacked = jnp.concatenate(
        [
            turn(queries[:, j * HD : (j + 1) * HD].astype(f32), cosine, sine)
            for j in range(group)
        ],
        axis=0,
    ).astype(jnp.bfloat16)

    def permutation(major, minor):
        size = major * minor
        to_row = lax.broadcasted_iota(jnp.int32, (size, size), 0)
        from_row = lax.broadcasted_iota(jnp.int32, (size, size), 1)
        wanted = (to_row % minor) * major + to_row // minor
        return jnp.where(wanted == from_row, 1.0, 0.0).astype(jnp.bfloat16)

    q_all[me] = jnp.dot(
        permutation(n_rows, group), stacked, preferred_element_type=f32
    ).astype(jnp.bfloat16)

    pl.semaphore_wait(barrier, 2 * n - 1)

    def q_copy(step):
        return pltpu.make_async_remote_copy(
            src_ref=q_all.at[me],
            dst_ref=q_all.at[me],
            send_sem=q_send.at[step],
            recv_sem=q_recv.at[me],
            device_id=to(peer_of(step), core),
            device_id_type=DEVICE,
        )

    def q_arrival(source):
        return pltpu.make_async_remote_copy(
            src_ref=q_all.at[source],
            dst_ref=q_all.at[source],
            send_sem=q_send.at[0],
            recv_sem=q_recv.at[source],
            device_id=to(source, core),
            device_id_type=DEVICE,
        )

    for step in range(1, n):
        q_copy(step).start()

    for which in range(2):
        for half in range(halves):
            scale_lanes[which, half] = jnp.concatenate(
                [
                    kv_scales[half * rows_half + r, which]
                    for r in range(rows_half)
                ],
                axis=1,
            ) * (score_scale if which == 0 else 1.0)
    shape = (rows_half * group, HD)
    row_of = lax.broadcasted_iota(jnp.int32, shape, 0) // group
    lane = lax.broadcasted_iota(jnp.int32, shape, 1)
    slot = me * block_len + lane % block_len
    masks = []
    for half in range(halves):
        live = jnp.zeros(shape, jnp.int32)
        for r in range(rows_half):
            live = jnp.where(row_of == r, lengths[half * rows_half + r], live)
        masks.append(
            jnp.where(
                (row_of == lane // block_len) & (slot < live), 0.0, NEG_FILL
            ).astype(f32)
        )

    fresh_pair = new_kv[me].astype(f32)
    angle_me = positions[me].astype(f32) * rates[...]
    cosine_me = jnp.cos(angle_me)
    sine_me = jnp.sin(angle_me) * sign
    fresh_keys = [
        turn(
            jnp.broadcast_to(fresh_pair[0:1, g * HD : (g + 1) * HD], (8, HD)),
            cosine_me,
            sine_me,
        )[0:1].astype(jnp.bfloat16).astype(f32)
        for g in range(n)
    ]
    fresh_values = [fresh_pair[1:2, g * HD : (g + 1) * HD] for g in range(n)]

    common = lax.broadcasted_iota(jnp.int32, (H, H), 0) & lax.broadcasted_iota(
        jnp.int32, (H, H), 1
    )
    parity = jnp.zeros((H, H), jnp.int32)
    for b in range(H.bit_length() - 1):
        parity = parity ^ (lax.shift_right_logical(common, b) & 1)
    sylvester = jnp.where(parity == 0, 1.0, -1.0).astype(jnp.bfloat16)

    kv_copy.wait()

    def attend(g, stats):
        lanes = pl.ds(pl.multiple_of(g * HD, HD), HD)
        result = []
        for half in range(halves):
            first = half * rows_half
            keys = kv_here[first : first + rows_half, 0, :, lanes].reshape(HD, HD)
            values = kv_here[first : first + rows_half, 1, :, lanes].reshape(HD, HD)
            query = q_all[g, half * shape[0] : (half + 1) * shape[0], :]
            raw = lax.dot_general(
                query, keys, (((1,), (1,)), ((), ())), preferred_element_type=f32
            )
            scores = raw * scale_lanes[0, half, pl.ds(g, 1), :] + masks[half]
            peak = jnp.maximum(jnp.max(scores, axis=1, keepdims=True), PEAK_FLOOR)
            weights = jnp.exp(scores - peak)
            total = jnp.sum(weights, axis=1, keepdims=True)
            weighted = weights * scale_lanes[1, half, pl.ds(g, 1), :]
            summed = jnp.dot(
                weighted.astype(jnp.bfloat16), values, preferred_element_type=f32
            ).astype(jnp.bfloat16)
            part_out[first : first + rows_half, g] = summed.reshape(
                rows_half, group, HD
            )
            stat = stats[half]
            stat = jnp.where(lane == g, peak, stat)
            result.append(jnp.where(lane == g + n, total, stat))
        return tuple(result)

    stats = attend(me, tuple(jnp.zeros(shape, f32) for _ in range(halves)))

    def attend_step(step, stats):
        g = peer_of(step)
        q_arrival(g).wait_recv()
        return attend(g, stats)

    stats = lax.fori_loop(1, n, attend_step, stats)
    for half in range(halves):
        stat_out[half * rows_half : (half + 1) * rows_half] = stats[half].reshape(
            rows_half, group, HD
        )

    def part_copy(step):
        return pltpu.make_async_remote_copy(
            src_ref=part_out.at[peer_of(step)],
            dst_ref=part_in.at[me],
            send_sem=part_send.at[step],
            recv_sem=part_recv.at[me],
            device_id=to(peer_of(step), core),
            device_id_type=DEVICE,
        )

    def stat_copy(step):
        return pltpu.make_async_remote_copy(
            src_ref=stat_out.at[peer_of(step)],
            dst_ref=stat_in.at[me],
            send_sem=stat_send.at[step],
            recv_sem=stat_recv.at[me],
            device_id=to(peer_of(step), core),
            device_id_type=DEVICE,
        )

    def part_arrival(source):
        return pltpu.make_async_remote_copy(
            src_ref=part_out.at[source],
            dst_ref=part_in.at[source],
            send_sem=part_send.at[0],
            recv_sem=part_recv.at[source],
            device_id=to(source, core),
            device_id_type=DEVICE,
        )

    def stat_arrival(source):
        return pltpu.make_async_remote_copy(
            src_ref=stat_out.at[source],
            dst_ref=stat_in.at[source],
            send_sem=stat_send.at[0],
            recv_sem=stat_recv.at[source],
            device_id=to(source, core),
            device_id_type=DEVICE,
        )

    for step in range(1, n):
        stat_copy(step).start()
        part_copy(step).start()
    part_in[me] = part_out[me]
    stat_in[me] = stat_out[me]

    lane_g = lax.broadcasted_iota(jnp.int32, (group, HD), 1)
    fresh = jnp.zeros((group, HD), f32)
    own_rows = pl.ds(pl.multiple_of(me * group, group), group)
    for g in range(n):
        score = jnp.sum(
            q_all[g, own_rows, :].astype(f32) * fresh_keys[g], axis=1, keepdims=True
        )
        fresh = jnp.where(lane_g == g, score * score_scale, fresh)

    for step in range(1, n):
        stat_arrival(peer_of(step)).wait_recv()
    stat = [stat_in[s] for s in range(n)]
    top = fresh
    for s in range(n):
        top = jnp.maximum(top, stat[s])
    factor = [jnp.exp(stat[s] - top) for s in range(n)]
    fresh_factor = jnp.exp(fresh - top)
    total = fresh_factor
    for s in range(n):
        total = total + factor[s] * pltpu.roll(stat[s], HD - n, 1)
    inverse = 1.0 / total
    factor = [f * inverse for f in factor]
    fresh_factor = fresh_factor * inverse

    for step in range(1, n):
        part_arrival(peer_of(step)).wait_recv()
    attended = []
    for g in range(n):
        mixed = fresh_factor[:, g : g + 1] * fresh_values[g]
        for s in range(n):
            mixed = mixed + factor[s][:, g : g + 1] * part_in[s, g].astype(f32)
        attended.append(mixed)
    attended = jnp.concatenate(attended, axis=0).astype(jnp.bfloat16)
    rotated = jnp.dot(sylvester, attended, preferred_element_type=f32) * (H ** (-0.5))
    rot_out[...] = rotated.astype(jnp.bfloat16).reshape(n, group, HD)

    def rot_copy(step, other):
        peer = peer_of(step)
        return pltpu.make_async_remote_copy(
            src_ref=rot_out.at[peer],
            dst_ref=rot_in.at[core, me],
            send_sem=rot_send.at[step, other],
            recv_sem=rot_recv.at[core, me],
            device_id=to(peer, lax.rem(core + other, 2)),
            device_id_type=DEVICE,
        )

    def rot_arrival(step, other):
        source = peer_of(step)
        side = lax.rem(core + other, 2)
        return pltpu.make_async_remote_copy(
            src_ref=rot_out.at[source],
            dst_ref=rot_in.at[side, source],
            send_sem=rot_send.at[0, 0],
            recv_sem=rot_recv.at[side, source],
            device_id=to(source, side),
            device_id_type=DEVICE,
        )

    pairs = [(s, o) for s in range(n) for o in range(2) if s or o]
    for step, other in pairs:
        rot_copy(step, other).start()
    rot_in[core, me] = rot_out[me]
    order = permutation(group, 2 * n_rows)
    for step, other in pairs:
        rot_arrival(step, other).wait_recv()
    tiles = jnp.dot(
        order, rot_in[...].reshape(2 * n_rows * group, HD), preferred_element_type=f32
    ).astype(jnp.bfloat16)
    flat_rows = jnp.concatenate(
        [tiles[k * 2 * n_rows : (k + 1) * 2 * n_rows] for k in range(group)], axis=1
    )

    def share_copy(i, other):
        side = lax.rem(core + other, 2)
        return pltpu.make_async_remote_copy(
            src_ref=share_out.at[i, side],
            dst_ref=share_in.at[core, me],
            send_sem=share_send.at[i, side],
            recv_sem=share_recv.at[core, me],
            device_id=to(i, side),
            device_id_type=DEVICE,
        )

    def share_arrival(step, other):
        source = peer_of(step)
        side = lax.rem(core + other, 2)
        return pltpu.make_async_remote_copy(
            src_ref=share_out.at[0, 0],
            dst_ref=share_in.at[side, source],
            send_sem=share_send.at[0, 0],
            recv_sem=share_recv.at[side, source],
            device_id=to(source, side),
            device_id_type=DEVICE,
        )

    def project(i):
        wo_copy(i).wait()
        share = jnp.dot(flat_rows, wo_here[i], preferred_element_type=f32)
        for side in range(2):
            rows = share[side * n_rows : (side + 1) * n_rows]
            share_out[i, side] = jnp.concatenate(
                [rows[:, :half_wide], rows[:, half_wide:]], axis=0
            ).astype(jnp.bfloat16)

    def project_step(step, carry):
        i = peer_of(step)
        project(i)
        share_copy(i, 0).start()
        share_copy(i, 1).start()
        return carry

    lax.fori_loop(1, n, project_step, 0)
    project(me)
    share_copy(me, 1).start()
    share_in[core, me] = share_out[me, core]

    for step, other in pairs:
        share_arrival(step, other).wait_recv()
    for side in range(2):
        added = share_in[side, 0].astype(f32)
        for s in range(1, n):
            added = added + share_in[side, s].astype(f32)
        for half in range(2):
            first = side * wide + half * half_wide
            columns = slice(first, first + half_wide)
            out[:, columns] = (
                residual[:, columns].astype(f32)
                + added[half * n_rows : (half + 1) * n_rows] * wo_scales[:, columns]
            ).astype(out.dtype)

    for step in range(1, n):
        q_copy(step).wait_send()
        stat_copy(step).wait_send()
        part_copy(step).wait_send()
    for step, other in pairs:
        rot_copy(step, other).wait_send()
        share_copy(peer_of(step), other).wait_send()


def on_device_fused(
    queries, new_kv, positions, lengths, kv_codes, kv_scales, wo_codes, wo_scales, residual
):
    n = lax.axis_size("head")
    n_rows = queries.shape[0]
    group = queries.shape[1] // HD
    block_len = kv_codes.shape[2]
    width = wo_codes.shape[1]
    wide = width // n // 2
    halves = n_rows * block_len // HD
    rates = ROPE_BASE ** (-(jnp.arange(HD // 2, dtype=jnp.float32) * (2.0 / HD)))
    rates = jnp.tile(rates, 2)[None, :]
    bf16, f32 = jnp.bfloat16, jnp.float32
    smem = pl.BlockSpec(memory_space=pltpu.SMEM)
    vmem = pl.BlockSpec(memory_space=pltpu.VMEM)
    hbm = pl.BlockSpec(memory_space=pl.ANY)
    dma = pltpu.SemaphoreType.DMA
    return pl.pallas_call(
        functools.partial(fused_kernel, n),
        out_shape=jax.ShapeDtypeStruct(residual.shape, bf16),
        in_specs=[smem, smem, vmem, vmem, vmem, vmem, vmem, vmem, hbm, hbm],
        out_specs=vmem,
        scratch_shapes=[
            pltpu.VMEM((n, n_rows * group, HD), bf16),
            pltpu.VMEM(kv_codes.shape, bf16),
            pltpu.VMEM((2, halves, KVH, HD), f32),
            pltpu.VMEM((n, n, group, HD), bf16),
            pltpu.VMEM((n, n, group, HD), bf16),
            pltpu.VMEM((n, group, HD), f32),
            pltpu.VMEM((n, group, HD), f32),
            pltpu.VMEM((n, group, HD), bf16),
            pltpu.VMEM((2, n, group, HD), bf16),
            pltpu.VMEM((n, wo_codes.shape[0], wide), bf16),
            pltpu.VMEM((n, 2, 2 * n_rows, wide // 2), bf16),
            pltpu.VMEM((2, n, 2 * n_rows, wide // 2), bf16),
            dma,
            dma((n,)),
            dma((n,)),
            dma((n,)),
            dma((n,)),
            dma((n,)),
            dma((n,)),
            dma((n,)),
            dma((n, 2)),
            dma((2, n)),
            dma((n, 2)),
            dma((2, n)),
        ],
        compiler_params=pltpu.CompilerParams(
            collective_id=0, has_side_effects=True, vmem_limit_bytes=48 * 1024 * 1024
        ),
        cost_estimate=pl.CostEstimate(
            flops=2 * 2 * n_rows * wo_codes.shape[0] * width // 2,
            bytes_accessed=wo_codes.shape[0] * width,
            transcendentals=0,
        ),
    )(
        positions,
        lengths,
        queries,
        new_kv,
        rates,
        residual,
        wo_scales[None, :],
        kv_scales,
        kv_codes,
        wo_codes,
    )


def on_device(*arrays):
    queries, kv_codes, wo_codes = arrays[0], arrays[4], arrays[6]
    n = lax.axis_size("head")
    n_rows, group, block_len = queries.shape[0], queries.shape[1] // HD, kv_codes.shape[2]
    fits = (
        lax.axis_size("dp") == 2
        and n == KVH == n_rows
        and group == H // KVH == 16
        and block_len % 16 == 0
        and block_len < HD
        and HD % block_len == 0
        and n_rows * block_len % HD == 0
        and wo_codes.shape[1] % (n * 512) == 0
    )
    return (on_device_fused if fits else on_device_general)(*arrays)


def solution(mesh):
    placed = (
        P(("group", "dp"), "head"),
        P(("group", "dp"), None, None),
        P(("group", "dp")),
        P(("group", "dp")),
        P(("group", "dp"), None, "head", None),
        P(("group", "dp"), None, None, "head"),
        P("head", None),
        P("head"),
        P(("group", "dp"), "head"),
    )
    return jax.shard_map(
        on_device, mesh=mesh, in_specs=placed, out_specs=P(("group", "dp"), "head"), check_vma=False
    )
```

```python
import functools
import math

import jax
import jax.numpy as jnp
from jax import lax
from jax.experimental import pallas as pl
from jax.experimental.pallas import tpu as pltpu
from jax.sharding import PartitionSpec as P

H = 128
KVH = 8
HD = 128


ROPE_BASE = 500000.0
NEG_FILL = -1e30


def partner_2(block, axis, distance):
    count = lax.axis_size(axis)
    route = []
    for low in range(count):
        high = low | 1 << distance
        if high != low and high < count:
            route += [(low, high), (high, low)]
    return lax.ppermute(block, axis, route)


def rotary(values_in, positions):
    half_dim = values_in.shape[-1] // 2
    inverse_rate = ROPE_BASE ** (
        -(jnp.arange(half_dim, dtype=jnp.float32) * (2.0 / values_in.shape[-1]))
    )
    angles = positions.astype(jnp.float32)[:, None, None] * inverse_rate
    cosine = jnp.cos(angles)
    sine_part = jnp.sin(angles)
    lower_half = values_in[..., :half_dim]
    upper_half = values_in[..., half_dim:]
    return jnp.concatenate(
        [
            lower_half * cosine - upper_half * sine_part,
            upper_half * cosine + lower_half * sine_part,
        ],
        axis=-1,
    )


def hadamard(size_needed):
    index_row = jnp.arange(size_needed, dtype=jnp.int32)
    common = jnp.bitwise_and(index_row[:, None], index_row[None, :])
    parity = jnp.zeros_like(common)
    for bit_pos in range(max(size_needed.bit_length() - 1, 0)):
        parity = parity + jnp.right_shift(common, bit_pos) % 2
    return jnp.where(parity % 2 == 0, 1.0, -1.0).astype(jnp.float32)


def settle(peak_source, total_source, summed_source, fresh_score, fresh_values):
    peak_final = jnp.maximum(jnp.max(peak_source, axis=1), fresh_score)
    rescale = jnp.exp(peak_source - peak_final[:, None])
    fresh_weight = jnp.exp(fresh_score - peak_final)
    total_final = jnp.sum(total_source * rescale, axis=1) + fresh_weight
    summed_final = (
        jnp.sum(summed_source * rescale[..., None], axis=1) + fresh_weight[..., None] * fresh_values
    )
    return (summed_final / total_final[..., None]).astype(jnp.bfloat16)


def on_device_general(
    queries, new_kv, positions, lengths, kv_codes, kv_scales, wo_codes, wo_scales, residual
):
    n_head = lax.axis_size("head")
    my_index = lax.axis_index("head")
    n_rows = queries.shape[0]
    heads_here = queries.shape[1] // HD
    group_size = H // KVH
    block_len = kv_codes.shape[2]
    first_slot = my_index * block_len
    score_scale = HD ** (-0.5)
    own_query = rotary(
        queries.reshape(n_rows, heads_here, HD).astype(jnp.float32), positions
    ).astype(jnp.bfloat16)
    all_query = lax.all_gather(
        own_query.reshape(n_rows, heads_here * HD), "head", axis=1, tiled=True
    )
    all_query = all_query.reshape(n_rows, KVH, group_size, HD)
    fresh_keys = rotary(
        new_kv[:, 0].reshape(n_rows, KVH, HD).astype(jnp.float32), positions
    ).astype(jnp.bfloat16)
    fresh_values = new_kv[:, 1].reshape(n_rows, KVH, HD).astype(jnp.float32)
    key_codes = kv_codes[:, 0].reshape(n_rows, block_len, KVH, HD)
    value_codes = kv_codes[:, 1].reshape(n_rows, block_len, KVH, HD).astype(jnp.float32)
    raw_scores = jnp.einsum(
        "rgjd,rtgd->rgjt", all_query, key_codes, preferred_element_type=jnp.float32
    )
    scores = raw_scores * kv_scales[:, 0][:, :, None, :] * score_scale
    slot_index = first_slot + jnp.arange(block_len, dtype=jnp.int32)
    is_valid = (slot_index[None, :] < lengths[:, None])[:, None, None, :]
    scores = jnp.where(is_valid, scores, NEG_FILL)
    peak_here = jnp.max(scores, axis=-1)
    weights = jnp.where(is_valid, jnp.exp(scores - peak_here[..., None]), 0.0)
    total_here = jnp.sum(weights, axis=-1)
    summed = jnp.einsum(
        "rgjt,rtgd->rgjd",
        weights * kv_scales[:, 1][:, :, None, :],
        value_codes,
        precision=lax.Precision.HIGHEST,
    )
    peak_full = peak_here.reshape(n_rows, H)
    total_full = total_here.reshape(n_rows, H)
    summed_full = summed.reshape(n_rows, H, HD)
    received = (
        lax.all_to_all(peak_full, "head", split_axis=1, concat_axis=1, tiled=True),
        lax.all_to_all(total_full, "head", split_axis=1, concat_axis=1, tiled=True),
        lax.all_to_all(summed_full, "head", split_axis=1, concat_axis=1, tiled=True),
    )
    peak_source = received[0].reshape(n_rows, n_head, heads_here)
    total_source = received[1].reshape(n_rows, n_head, heads_here)
    summed_source = received[2].reshape(n_rows, n_head, heads_here, HD)
    owned_group = my_index * heads_here // group_size
    key_owned = lax.dynamic_index_in_dim(fresh_keys, owned_group, 1, keepdims=False)
    fresh_score = (
        jnp.einsum("rjd,rd->rj", own_query, key_owned, preferred_element_type=jnp.float32)
        * score_scale
    )
    value_owned = lax.dynamic_index_in_dim(fresh_values, owned_group, 1, keepdims=False)
    fresh_spread = jnp.broadcast_to(value_owned[:, None, :], (n_rows, heads_here, HD))
    attended = settle(peak_source, total_source, summed_source, fresh_score, fresh_spread)
    local_table = hadamard(heads_here)
    rotated = jnp.einsum(
        "kj,rjd->rkd", local_table, attended.astype(jnp.float32), precision=lax.Precision.HIGHEST
    )
    for bit_pos in range(n_head.bit_length() - 1):
        partner = partner_2(rotated, "head", bit_pos)
        is_upper = jnp.right_shift(my_index, bit_pos) % 2 == 1
        rotated = jnp.where(is_upper, partner - rotated, rotated + partner)
    flat_rows = (rotated * H ** (-0.5)).reshape(n_rows, heads_here * HD).astype(jnp.bfloat16)
    partial_out = jnp.dot(flat_rows, wo_codes, preferred_element_type=jnp.float32)
    shares = lax.psum_scatter(partial_out, "head", scatter_dimension=1, tiled=True)
    return (residual.astype(jnp.float32) + shares * wo_scales).astype(jnp.bfloat16)


PEAK_FLOOR = -1e29
DEVICE = pl.DeviceIdType.MESH


def fused_kernel(
    n,
    positions_far,
    lengths_far,
    rates_far,
    queries_far,
    new_kv_far,
    kv_scales_far,
    residual_far,
    wo_scales_far,
    kv_codes,
    wo_codes,
    out,
    positions,
    lengths,
    rates,
    queries,
    new_kv,
    kv_scales,
    residual,
    wo_scales,
    in_sem,
    q_all,
    kv_here,
    scale_lanes,
    part_out,
    part_in,
    stat_out,
    stat_in,
    rot_out,
    rot_in,
    wo_here,
    share_out,
    share_in,
    kv_sem,
    wo_sem,
    q_send,
    q_recv,
    part_send,
    part_recv,
    stat_send,
    stat_recv,
    rot_send,
    rot_recv,
    share_send,
    share_recv,
):
    me = lax.axis_index("head")
    core = lax.axis_index("dp")
    n_rows = queries.shape[0]
    group = queries.shape[1] // HD
    block_len = kv_codes.shape[2]
    wide = wo_here.shape[2]
    half_wide = wide // 2
    halves = n_rows * block_len // HD
    rows_half = n_rows // halves
    score_scale = HD ** (-0.5)
    f32 = jnp.float32

    def peer_of(step):
        peer = 0
        for b in range(n.bit_length() - 1):
            peer += ((me // 2**b + step // 2**b) % 2) * 2**b
        return peer

    def to(head, dp):
        return {"head": head, "dp": dp}

    fetched = [
        pltpu.make_async_copy(far, near, in_sem.at[k])
        for k, (far, near) in enumerate(
            [
                (positions_far, positions),
                (rates_far, rates),
                (queries_far, queries),
                (lengths_far, lengths),
                (kv_scales_far, kv_scales),
                (new_kv_far, new_kv),
                (residual_far, residual),
                (wo_scales_far, wo_scales),
            ]
        )
    ]
    for copy in fetched:
        copy.start()
    kv_copy = pltpu.make_async_copy(kv_codes, kv_here, kv_sem)
    kv_copy.start()

    def wo_copy(i):
        first = pl.multiple_of(i * (2 * wide) + core * wide, wide)
        return pltpu.make_async_copy(
            wo_codes.at[:, pl.ds(first, wide)], wo_here.at[i], wo_sem.at[i]
        )

    for step in reversed(range(n)):
        wo_copy(peer_of(step)).start()

    barrier = pltpu.get_barrier_semaphore()
    for step in range(n):
        for other in range(2):
            if step or other:
                pl.semaphore_signal(
                    barrier,
                    inc=1,
                    device_id=to(peer_of(step), lax.rem(core + other, 2)),
                    device_id_type=DEVICE,
                )

    lane_1 = lax.broadcasted_iota(jnp.int32, (1, HD), 1)
    row_8 = lax.broadcasted_iota(jnp.int32, (n_rows, HD), 0)
    for copy in fetched[:3]:
        copy.wait()
    pos = jnp.zeros((n_rows, HD), f32)
    for r in range(n_rows):
        pos = jnp.where(row_8 == r, positions[r].astype(f32), pos)
    sign = jnp.where(lane_1 < HD // 2, -1.0, 1.0).astype(f32)
    angle = pos * rates[...]
    cosine = jnp.cos(angle)
    sine = jnp.sin(angle) * sign

    def turn(v, c, s):
        return v * c + pltpu.roll(v, HD // 2, 1) * s

    stacked = jnp.concatenate(
        [
            turn(queries[:, j * HD : (j + 1) * HD].astype(f32), cosine, sine)
            for j in range(group)
        ],
        axis=0,
    ).astype(jnp.bfloat16)

    def permutation(major, minor):
        size = major * minor
        to_row = lax.broadcasted_iota(jnp.int32, (size, size), 0)
        from_row = lax.broadcasted_iota(jnp.int32, (size, size), 1)
        wanted = (to_row % minor) * major + to_row // minor
        return jnp.where(wanted == from_row, 1.0, 0.0).astype(jnp.bfloat16)

    q_all[me] = jnp.dot(
        permutation(n_rows, group), stacked, preferred_element_type=f32
    ).astype(jnp.bfloat16)

    pl.semaphore_wait(barrier, 2 * n - 1)

    def q_copy(step):
        return pltpu.make_async_remote_copy(
            src_ref=q_all.at[me],
            dst_ref=q_all.at[me],
            send_sem=q_send.at[step],
            recv_sem=q_recv.at[me],
            device_id=to(peer_of(step), core),
            device_id_type=DEVICE,
        )

    def q_forward(step):
        block = peer_of(step)
        return pltpu.make_async_remote_copy(
            src_ref=q_all.at[block],
            dst_ref=q_all.at[block],
            send_sem=q_send.at[step + 1],
            recv_sem=q_recv.at[block],
            device_id=to(peer_of(1), core),
            device_id_type=DEVICE,
        )

    def q_arrival(source):
        return pltpu.make_async_remote_copy(
            src_ref=q_all.at[source],
            dst_ref=q_all.at[source],
            send_sem=q_send.at[0],
            recv_sem=q_recv.at[source],
            device_id=to(source, core),
            device_id_type=DEVICE,
        )

    direct = [1] + list(range(2, n, 2))
    for step in direct:
        q_copy(step).start()
    for copy in fetched[3:6]:
        copy.wait()

    for which in range(2):
        for half in range(halves):
            scale_lanes[which, half] = jnp.concatenate(
                [
                    kv_scales[half * rows_half + r, which]
                    for r in range(rows_half)
                ],
                axis=1,
            ) * (score_scale if which == 0 else 1.0)
    shape = (rows_half * group, HD)
    row_of = lax.broadcasted_iota(jnp.int32, shape, 0) // group
    lane = lax.broadcasted_iota(jnp.int32, shape, 1)
    slot = me * block_len + lane % block_len
    masks = []
    for half in range(halves):
        live = jnp.zeros(shape, jnp.int32)
        for r in range(rows_half):
            live = jnp.where(row_of == r, lengths[half * rows_half + r], live)
        masks.append(
            jnp.where(
                (row_of == lane // block_len) & (slot < live), 0.0, NEG_FILL
            ).astype(f32)
        )

    fresh_pair = new_kv[me].astype(f32)
    angle_me = positions[me].astype(f32) * rates[...]
    cosine_me = jnp.cos(angle_me)
    sine_me = jnp.sin(angle_me) * sign
    fresh_keys = [
        turn(
            jnp.broadcast_to(fresh_pair[0:1, g * HD : (g + 1) * HD], (8, HD)),
            cosine_me,
            sine_me,
        )[0:1].astype(jnp.bfloat16).astype(f32)
        for g in range(n)
    ]
    fresh_values = [fresh_pair[1:2, g * HD : (g + 1) * HD] for g in range(n)]

    common = lax.broadcasted_iota(jnp.int32, (H, H), 0) & lax.broadcasted_iota(
        jnp.int32, (H, H), 1
    )
    parity = jnp.zeros((H, H), jnp.int32)
    for b in range(H.bit_length() - 1):
        parity = parity ^ (lax.shift_right_logical(common, b) & 1)
    sylvester = jnp.where(parity == 0, 1.0, -1.0).astype(jnp.bfloat16)

    kv_copy.wait()

    def attend(g, stats):
        lanes = pl.ds(pl.multiple_of(g * HD, HD), HD)
        result = []
        for half in range(halves):
            first = half * rows_half
            keys = kv_here[first : first + rows_half, 0, :, lanes].reshape(HD, HD)
            values = kv_here[first : first + rows_half, 1, :, lanes].reshape(HD, HD)
            query = q_all[g, half * shape[0] : (half + 1) * shape[0], :]
            raw = lax.dot_general(
                query, keys, (((1,), (1,)), ((), ())), preferred_element_type=f32
            )
            scores = raw * scale_lanes[0, half, pl.ds(g, 1), :] + masks[half]
            peak = jnp.maximum(jnp.max(scores, axis=1, keepdims=True), PEAK_FLOOR)
            weights = jnp.exp(scores - peak)
            total = jnp.sum(weights, axis=1, keepdims=True)
            weighted = weights * scale_lanes[1, half, pl.ds(g, 1), :]
            summed = jnp.dot(
                weighted.astype(jnp.bfloat16), values, preferred_element_type=f32
            ).astype(jnp.bfloat16)
            part_out[first : first + rows_half, g] = summed.reshape(
                rows_half, group, HD
            )
            stat = stats[half]
            stat = jnp.where(lane == g, peak, stat)
            result.append(jnp.where(lane == g + n, total, stat))
        return tuple(result)

    def part_copy(step, first=0, count=n):
        return pltpu.make_async_remote_copy(
            src_ref=part_out.at[peer_of(step), pl.ds(first, count)],
            dst_ref=part_in.at[me, pl.ds(first, count)],
            send_sem=part_send.at[step],
            recv_sem=part_recv.at[me],
            device_id=to(peer_of(step), core),
            device_id_type=DEVICE,
        )

    def stat_copy(step):
        return pltpu.make_async_remote_copy(
            src_ref=stat_out.at[peer_of(step)],
            dst_ref=stat_in.at[me],
            send_sem=stat_send.at[step],
            recv_sem=stat_recv.at[me],
            device_id=to(peer_of(step), core),
            device_id_type=DEVICE,
        )

    def part_arrival(source):
        return pltpu.make_async_remote_copy(
            src_ref=part_out.at[source],
            dst_ref=part_in.at[source],
            send_sem=part_send.at[0],
            recv_sem=part_recv.at[source],
            device_id=to(source, core),
            device_id_type=DEVICE,
        )

    def stat_arrival(source):
        return pltpu.make_async_remote_copy(
            src_ref=stat_out.at[source],
            dst_ref=stat_in.at[source],
            send_sem=stat_send.at[0],
            recv_sem=stat_recv.at[source],
            device_id=to(source, core),
            device_id_type=DEVICE,
        )

    def send_part(step):
        first = peer_of(step) // 2 * 2
        for s in reversed(range(1, n)):
            part_copy(s, first, 2).start()

    def await_q(step):
        q_arrival(peer_of(step)).wait_recv()

    stats = attend(me, tuple(jnp.zeros(shape, f32) for _ in range(halves)))
    for step in range(1, n, 2):
        if step + 1 < n:
            await_q(step + 1)
            q_forward(step + 1).start()
        await_q(step)
        stats = attend(peer_of(step), stats)
        if step + 1 < n:
            stats = attend(peer_of(step + 1), stats)
        else:
            for half in range(halves):
                for r in range(rows_half):
                    upper = stats[half][r * group : r * group + group // 2]
                    lower = stats[half][r * group + group // 2 : (r + 1) * group]
                    stat_out[half * rows_half + r] = upper + pltpu.roll(lower, 2 * n, 1)
            for s in reversed(range(1, n)):
                stat_copy(s).start()
        send_part(step)
    part_in[me] = part_out[me]
    stat_in[me] = stat_out[me]

    lane_g = lax.broadcasted_iota(jnp.int32, (group, HD), 1)
    fresh = jnp.zeros((group, HD), f32)
    own_rows = pl.ds(pl.multiple_of(me * group, group), group)
    for g in range(n):
        score = jnp.sum(
            q_all[g, own_rows, :].astype(f32) * fresh_keys[g], axis=1, keepdims=True
        )
        fresh = jnp.where(lane_g == g, score * score_scale, fresh)

    for step in range(1, n):
        stat_arrival(peer_of(step)).wait_recv()
    stat = []
    for s in range(n):
        packed = stat_in[s]
        stat.append(
            jnp.concatenate([packed, pltpu.roll(packed, HD - 2 * n, 1)], axis=0)
        )
    top = fresh
    for s in range(n):
        top = jnp.maximum(top, stat[s])
    factor = [jnp.exp(stat[s] - top) for s in range(n)]
    fresh_factor = jnp.exp(fresh - top)
    total = fresh_factor
    for s in range(n):
        total = total + factor[s] * pltpu.roll(stat[s], HD - n, 1)
    inverse = 1.0 / total
    factor = [f * inverse for f in factor]
    fresh_factor = fresh_factor * inverse

    for step in range(1, n):
        part_arrival(peer_of(step)).wait_recv()
    attended = []
    for g in range(n):
        mixed = fresh_factor[:, g : g + 1] * fresh_values[g]
        for s in range(n):
            mixed = mixed + factor[s][:, g : g + 1] * part_in[s, g].astype(f32)
        attended.append(mixed)
    attended = jnp.concatenate(attended, axis=0).astype(jnp.bfloat16)
    rotated = jnp.dot(sylvester, attended, preferred_element_type=f32) * (H ** (-0.5))
    rot_out[...] = rotated.astype(jnp.bfloat16).reshape(n, group, HD)

    def rot_copy(step, other):
        peer = peer_of(step)
        return pltpu.make_async_remote_copy(
            src_ref=rot_out.at[peer],
            dst_ref=rot_in.at[core, me],
            send_sem=rot_send.at[step, other],
            recv_sem=rot_recv.at[core, me],
            device_id=to(peer, lax.rem(core + other, 2)),
            device_id_type=DEVICE,
        )

    def rot_arrival(step, other):
        source = peer_of(step)
        side = lax.rem(core + other, 2)
        return pltpu.make_async_remote_copy(
            src_ref=rot_out.at[source],
            dst_ref=rot_in.at[side, source],
            send_sem=rot_send.at[0, 0],
            recv_sem=rot_recv.at[side, source],
            device_id=to(source, side),
            device_id_type=DEVICE,
        )

    pairs = [(s, o) for s in range(n) for o in range(2) if s or o]
    for step, other in pairs:
        rot_copy(step, other).start()
    rot_in[core, me] = rot_out[me]
    order = permutation(group, 2 * n_rows)
    for step, other in pairs:
        rot_arrival(step, other).wait_recv()
    tiles = jnp.dot(
        order, rot_in[...].reshape(2 * n_rows * group, HD), preferred_element_type=f32
    ).astype(jnp.bfloat16)
    flat_rows = jnp.concatenate(
        [tiles[k * 2 * n_rows : (k + 1) * 2 * n_rows] for k in range(group)], axis=1
    )

    def share_copy(i, other):
        side = lax.rem(core + other, 2)
        return pltpu.make_async_remote_copy(
            src_ref=share_out.at[i, side],
            dst_ref=share_in.at[core, me],
            send_sem=share_send.at[i, side],
            recv_sem=share_recv.at[core, me],
            device_id=to(i, side),
            device_id_type=DEVICE,
        )

    def share_arrival(step, other):
        source = peer_of(step)
        side = lax.rem(core + other, 2)
        return pltpu.make_async_remote_copy(
            src_ref=share_out.at[0, 0],
            dst_ref=share_in.at[side, source],
            send_sem=share_send.at[0, 0],
            recv_sem=share_recv.at[side, source],
            device_id=to(source, side),
            device_id_type=DEVICE,
        )

    def project(i):
        wo_copy(i).wait()
        share = jnp.dot(flat_rows, wo_here[i], preferred_element_type=f32)
        for side in range(2):
            rows = share[side * n_rows : (side + 1) * n_rows]
            share_out[i, side] = jnp.concatenate(
                [rows[:, :half_wide], rows[:, half_wide:]], axis=0
            ).astype(jnp.bfloat16)

    def project_step(step, carry):
        i = peer_of(n - step)
        project(i)
        share_copy(i, 0).start()
        share_copy(i, 1).start()
        return carry

    lax.fori_loop(1, n, project_step, 0)
    project(me)
    share_copy(me, 1).start()
    share_in[core, me] = share_out[me, core]

    for copy in fetched[6:]:
        copy.wait()
    for step, other in pairs:
        share_arrival(step, other).wait_recv()
    for side in range(2):
        added = share_in[side, 0].astype(f32)
        for s in range(1, n):
            added = added + share_in[side, s].astype(f32)
        for half in range(2):
            first = side * wide + half * half_wide
            columns = slice(first, first + half_wide)
            out[:, columns] = (
                residual[:, columns].astype(f32)
                + added[half * n_rows : (half + 1) * n_rows] * wo_scales[:, columns]
            ).astype(out.dtype)

    for step in direct:
        q_copy(step).wait_send()
    for step in direct[1:]:
        q_forward(step).wait_send()
    for step in range(1, n):
        stat_copy(step).wait_send()
        part_copy(step).wait_send()
    for step, other in pairs:
        rot_copy(step, other).wait_send()
        share_copy(peer_of(step), other).wait_send()


def on_device_fused(
    queries, new_kv, positions, lengths, kv_codes, kv_scales, wo_codes, wo_scales, residual
):
    n = lax.axis_size("head")
    n_rows = queries.shape[0]
    group = queries.shape[1] // HD
    block_len = kv_codes.shape[2]
    width = wo_codes.shape[1]
    wide = width // n // 2
    halves = n_rows * block_len // HD
    rates = ROPE_BASE ** (-(jnp.arange(HD // 2, dtype=jnp.float32) * (2.0 / HD)))
    rates = jnp.tile(rates, 2)[None, :]
    bf16, f32 = jnp.bfloat16, jnp.float32
    vmem = pl.BlockSpec(memory_space=pltpu.VMEM)
    hbm = pl.BlockSpec(memory_space=pltpu.HBM)
    dma = pltpu.SemaphoreType.DMA
    return pl.pallas_call(
        functools.partial(fused_kernel, n),
        out_shape=jax.ShapeDtypeStruct(residual.shape, bf16),
        in_specs=[hbm] * 10,
        out_specs=vmem,
        scratch_shapes=[
            pltpu.SMEM(positions.shape, jnp.int32),
            pltpu.SMEM(lengths.shape, jnp.int32),
            pltpu.VMEM(rates.shape, f32),
            pltpu.VMEM(queries.shape, bf16),
            pltpu.VMEM(new_kv.shape, bf16),
            pltpu.VMEM(kv_scales.shape, f32),
            pltpu.VMEM(residual.shape, bf16),
            pltpu.VMEM((1,) + wo_scales.shape, f32),
            dma((8,)),
            pltpu.VMEM((n, n_rows * group, HD), bf16),
            pltpu.VMEM(kv_codes.shape, bf16),
            pltpu.VMEM((2, halves, KVH, HD), f32),
            pltpu.VMEM((n, n, group, HD), bf16),
            pltpu.VMEM((n, n, group, HD), bf16),
            pltpu.VMEM((n, group // 2, HD), f32),
            pltpu.VMEM((n, group // 2, HD), f32),
            pltpu.VMEM((n, group, HD), bf16),
            pltpu.VMEM((2, n, group, HD), bf16),
            pltpu.VMEM((n, wo_codes.shape[0], wide), bf16),
            pltpu.VMEM((n, 2, 2 * n_rows, wide // 2), bf16),
            pltpu.VMEM((2, n, 2 * n_rows, wide // 2), bf16),
            dma,
            dma((n,)),
            dma((n,)),
            dma((n,)),
            dma((n,)),
            dma((n,)),
            dma((n,)),
            dma((n,)),
            dma((n, 2)),
            dma((2, n)),
            dma((n, 2)),
            dma((2, n)),
        ],
        compiler_params=pltpu.CompilerParams(
            collective_id=0, has_side_effects=True, vmem_limit_bytes=64 * 1024 * 1024
        ),
        cost_estimate=pl.CostEstimate(
            flops=2 * 2 * n_rows * wo_codes.shape[0] * width // 2,
            bytes_accessed=wo_codes.shape[0] * width,
            transcendentals=0,
        ),
    )(
        positions,
        lengths,
        rates,
        queries,
        new_kv,
        kv_scales,
        residual,
        wo_scales[None, :],
        kv_codes,
        wo_codes,
    )


def on_device(*arrays):
    queries, kv_codes, wo_codes = arrays[0], arrays[4], arrays[6]
    n = lax.axis_size("head")
    n_rows, group, block_len = queries.shape[0], queries.shape[1] // HD, kv_codes.shape[2]
    fits = (
        lax.axis_size("dp") == 2
        and n == KVH == n_rows
        and n & (n - 1) == 0
        and group == H // KVH == 16
        and block_len % 16 == 0
        and block_len < HD
        and HD % block_len == 0
        and n_rows * block_len % HD == 0
        and wo_codes.shape[1] % (n * 512) == 0
    )
    return (on_device_fused if fits else on_device_general)(*arrays)


def solution(mesh):
    placed = (
        P(("group", "dp"), "head"),
        P(("group", "dp"), None, None),
        P(("group", "dp")),
        P(("group", "dp")),
        P(("group", "dp"), None, "head", None),
        P(("group", "dp"), None, None, "head"),
        P("head", None),
        P("head"),
        P(("group", "dp"), "head"),
    )
    return jax.shard_map(
        on_device, mesh=mesh, in_specs=placed, out_specs=P(("group", "dp"), "head"), check_vma=False
    )
```

```python
import functools

import jax
import jax.numpy as jnp
import numpy as np
from jax import lax
from jax.experimental import pallas as pl
from jax.experimental.pallas import tpu as pltpu
from jax.sharding import PartitionSpec as P

H = 128
KVH = 8
HD = 128


ROPE_BASE = 500000.0
NEG_FILL = -1e30


def partner_2(block, axis, distance):
    count = lax.axis_size(axis)
    route = []
    for low in range(count):
        high = low | 1 << distance
        if high != low and high < count:
            route += [(low, high), (high, low)]
    return lax.ppermute(block, axis, route)


def rotary(values_in, positions):
    half_dim = values_in.shape[-1] // 2
    inverse_rate = ROPE_BASE ** (
        -(jnp.arange(half_dim, dtype=jnp.float32) * (2.0 / values_in.shape[-1]))
    )
    angles = positions.astype(jnp.float32)[:, None, None] * inverse_rate
    cosine = jnp.cos(angles)
    sine_part = jnp.sin(angles)
    lower_half = values_in[..., :half_dim]
    upper_half = values_in[..., half_dim:]
    return jnp.concatenate(
        [
            lower_half * cosine - upper_half * sine_part,
            upper_half * cosine + lower_half * sine_part,
        ],
        axis=-1,
    )


def hadamard(size_needed):
    index_row = jnp.arange(size_needed, dtype=jnp.int32)
    common = jnp.bitwise_and(index_row[:, None], index_row[None, :])
    parity = jnp.zeros_like(common)
    for bit_pos in range(max(size_needed.bit_length() - 1, 0)):
        parity = parity + jnp.right_shift(common, bit_pos) % 2
    return jnp.where(parity % 2 == 0, 1.0, -1.0).astype(jnp.float32)


def settle(peak_source, total_source, summed_source, fresh_score, fresh_values):
    peak_final = jnp.maximum(jnp.max(peak_source, axis=1), fresh_score)
    rescale = jnp.exp(peak_source - peak_final[:, None])
    fresh_weight = jnp.exp(fresh_score - peak_final)
    total_final = jnp.sum(total_source * rescale, axis=1) + fresh_weight
    summed_final = (
        jnp.sum(summed_source * rescale[..., None], axis=1) + fresh_weight[..., None] * fresh_values
    )
    return (summed_final / total_final[..., None]).astype(jnp.bfloat16)


def on_device_general(
    queries, new_kv, positions, lengths, kv_codes, kv_scales, wo_codes, wo_scales, residual
):
    n_head = lax.axis_size("head")
    my_index = lax.axis_index("head")
    n_rows = queries.shape[0]
    heads_here = queries.shape[1] // HD
    group_size = H // KVH
    block_len = kv_codes.shape[2]
    first_slot = my_index * block_len
    score_scale = HD ** (-0.5)
    own_query = rotary(
        queries.reshape(n_rows, heads_here, HD).astype(jnp.float32), positions
    ).astype(jnp.bfloat16)
    all_query = lax.all_gather(
        own_query.reshape(n_rows, heads_here * HD), "head", axis=1, tiled=True
    )
    all_query = all_query.reshape(n_rows, KVH, group_size, HD)
    fresh_keys = rotary(
        new_kv[:, 0].reshape(n_rows, KVH, HD).astype(jnp.float32), positions
    ).astype(jnp.bfloat16)
    fresh_values = new_kv[:, 1].reshape(n_rows, KVH, HD).astype(jnp.float32)
    key_codes = kv_codes[:, 0].reshape(n_rows, block_len, KVH, HD)
    value_codes = kv_codes[:, 1].reshape(n_rows, block_len, KVH, HD).astype(jnp.float32)
    raw_scores = jnp.einsum(
        "rgjd,rtgd->rgjt", all_query, key_codes, preferred_element_type=jnp.float32
    )
    scores = raw_scores * kv_scales[:, 0][:, :, None, :] * score_scale
    slot_index = first_slot + jnp.arange(block_len, dtype=jnp.int32)
    is_valid = (slot_index[None, :] < lengths[:, None])[:, None, None, :]
    scores = jnp.where(is_valid, scores, NEG_FILL)
    peak_here = jnp.max(scores, axis=-1)
    weights = jnp.where(is_valid, jnp.exp(scores - peak_here[..., None]), 0.0)
    total_here = jnp.sum(weights, axis=-1)
    summed = jnp.einsum(
        "rgjt,rtgd->rgjd",
        weights * kv_scales[:, 1][:, :, None, :],
        value_codes,
        precision=lax.Precision.HIGHEST,
    )
    peak_full = peak_here.reshape(n_rows, H)
    total_full = total_here.reshape(n_rows, H)
    summed_full = summed.reshape(n_rows, H, HD)
    received = (
        lax.all_to_all(peak_full, "head", split_axis=1, concat_axis=1, tiled=True),
        lax.all_to_all(total_full, "head", split_axis=1, concat_axis=1, tiled=True),
        lax.all_to_all(summed_full, "head", split_axis=1, concat_axis=1, tiled=True),
    )
    peak_source = received[0].reshape(n_rows, n_head, heads_here)
    total_source = received[1].reshape(n_rows, n_head, heads_here)
    summed_source = received[2].reshape(n_rows, n_head, heads_here, HD)
    owned_group = my_index * heads_here // group_size
    key_owned = lax.dynamic_index_in_dim(fresh_keys, owned_group, 1, keepdims=False)
    fresh_score = (
        jnp.einsum("rjd,rd->rj", own_query, key_owned, preferred_element_type=jnp.float32)
        * score_scale
    )
    value_owned = lax.dynamic_index_in_dim(fresh_values, owned_group, 1, keepdims=False)
    fresh_spread = jnp.broadcast_to(value_owned[:, None, :], (n_rows, heads_here, HD))
    attended = settle(peak_source, total_source, summed_source, fresh_score, fresh_spread)
    local_table = hadamard(heads_here)
    rotated = jnp.einsum(
        "kj,rjd->rkd", local_table, attended.astype(jnp.float32), precision=lax.Precision.HIGHEST
    )
    for bit_pos in range(n_head.bit_length() - 1):
        partner = partner_2(rotated, "head", bit_pos)
        is_upper = jnp.right_shift(my_index, bit_pos) % 2 == 1
        rotated = jnp.where(is_upper, partner - rotated, rotated + partner)
    flat_rows = (rotated * H ** (-0.5)).reshape(n_rows, heads_here * HD).astype(jnp.bfloat16)
    partial_out = jnp.dot(flat_rows, wo_codes, preferred_element_type=jnp.float32)
    shares = lax.psum_scatter(partial_out, "head", scatter_dimension=1, tiled=True)
    return (residual.astype(jnp.float32) + shares * wo_scales).astype(jnp.bfloat16)


PEAK_FLOOR = -1e29
DEVICE = pl.DeviceIdType.MESH


def fused_kernel(
    n,
    positions_far,
    lengths_far,
    rates_far,
    queries_far,
    new_kv_far,
    kv_scales_far,
    kv_codes,
    wo_codes,
    out,
    positions,
    lengths,
    rates,
    queries,
    new_kv,
    kv_scales,
    in_sem,
    q_all,
    kv_here,
    scale_lanes,
    part_out,
    part_in,
    stat_out,
    stat_in,
    rot_out,
    rot_in,
    wo_here,
    share_out,
    share_in,
    kv_sem,
    wo_sem,
    q_send,
    q_recv,
    part_send,
    part_recv,
    stat_send,
    stat_recv,
    rot_send,
    rot_recv,
    share_send,
    share_recv,
):
    me = lax.axis_index("head")
    core = lax.axis_index("dp")
    n_rows = queries.shape[0]
    group = queries.shape[1] // HD
    block_len = kv_codes.shape[2]
    wide = wo_here.shape[2]
    half_wide = wide // 2
    halves = n_rows * block_len // HD
    rows_half = n_rows // halves
    score_scale = HD ** (-0.5)
    f32 = jnp.float32

    n_bits = n.bit_length() - 1
    bits = [lax.rem(lax.div(me, 2**b), 2) for b in range(n_bits)]
    peers = [
        sum((1 - bits[b] if step >> b & 1 else bits[b]) * 2**b for b in range(n_bits))
        for step in range(n)
    ]
    other_core = 1 - core

    def peer_of(step):
        return peers[step]

    def peer_at(step):
        peer = 0
        for b in range(n_bits):
            bit = lax.rem(lax.div(step, 2**b), 2)
            peer += (bits[b] + bit - 2 * bits[b] * bit) * 2**b
        return peer

    def side_of(other):
        return other_core if other else core

    def to(head, dp):
        return {"head": head, "dp": dp}

    fetched = [
        pltpu.make_async_copy(far, near, in_sem.at[k])
        for k, (far, near) in enumerate(
            [
                (positions_far, positions),
                (rates_far, rates),
                (queries_far, queries),
                (lengths_far, lengths),
                (kv_scales_far, kv_scales),
                (new_kv_far, new_kv),
            ]
        )
    ]
    for copy in fetched:
        copy.start()
    kv_copy = pltpu.make_async_copy(kv_codes, kv_here, kv_sem)
    kv_copy.start()

    def wo_copy(i):
        first = pl.multiple_of(i * (2 * wide) + core * wide, wide)
        return pltpu.make_async_copy(
            wo_codes.at[:, pl.ds(first, wide)], wo_here.at[i], wo_sem.at[i]
        )

    barrier = pltpu.get_barrier_semaphore()
    for step in range(n):
        for other in range(2):
            if step or other:
                pl.semaphore_signal(
                    barrier,
                    inc=1,
                    device_id=to(peer_of(step), side_of(other)),
                    device_id_type=DEVICE,
                )

    lane_1 = lax.broadcasted_iota(jnp.int32, (1, HD), 1)
    row_8 = lax.broadcasted_iota(jnp.int32, (n_rows, HD), 0)
    for copy in fetched[:3]:
        copy.wait()
    pos = jnp.zeros((n_rows, HD), f32)
    for r in range(n_rows):
        pos = jnp.where(row_8 == r, positions[r].astype(f32), pos)
    sign = jnp.where(lane_1 < HD // 2, -1.0, 1.0).astype(f32)
    angle = pos * rates[...]
    cosine = jnp.cos(angle)
    sine = jnp.sin(angle) * sign

    def turn(v, c, s):
        return v * c + pltpu.roll(v, HD // 2, 1) * s

    stacked = jnp.concatenate(
        [
            turn(queries[:, j * HD : (j + 1) * HD].astype(f32), cosine, sine)
            for j in range(group)
        ],
        axis=0,
    ).astype(jnp.bfloat16)

    def permutation(major, minor):
        size = major * minor
        to_row = lax.broadcasted_iota(jnp.int32, (size, size), 0)
        from_row = lax.broadcasted_iota(jnp.int32, (size, size), 1)
        shift = minor.bit_length() - 1
        wanted = (to_row & (minor - 1)) * major + (to_row >> shift)
        return jnp.where(wanted == from_row, 1.0, 0.0).astype(jnp.bfloat16)

    q_all[me] = jnp.dot(
        permutation(n_rows, group), stacked, preferred_element_type=f32
    ).astype(jnp.bfloat16)

    pl.semaphore_wait(barrier, 2 * n - 1)

    def q_copy(step):
        return pltpu.make_async_remote_copy(
            src_ref=q_all.at[me],
            dst_ref=q_all.at[me],
            send_sem=q_send.at[step],
            recv_sem=q_recv.at[me],
            device_id=to(peer_of(step), core),
            device_id_type=DEVICE,
        )

    def q_forward(step):
        block = peer_of(step)
        return pltpu.make_async_remote_copy(
            src_ref=q_all.at[block],
            dst_ref=q_all.at[block],
            send_sem=q_send.at[step + 1],
            recv_sem=q_recv.at[block],
            device_id=to(peer_of(1), core),
            device_id_type=DEVICE,
        )

    def q_arrival(source):
        return pltpu.make_async_remote_copy(
            src_ref=q_all.at[source],
            dst_ref=q_all.at[source],
            send_sem=q_send.at[0],
            recv_sem=q_recv.at[source],
            device_id=to(source, core),
            device_id_type=DEVICE,
        )

    direct = [1] + list(range(2, n, 2))
    for step in direct:
        q_copy(step).start()
    for step in (n - 1, n - 2):
        wo_copy(peer_of(step)).start()
    for copy in fetched[3:]:
        copy.wait()

    for which in range(2):
        for half in range(halves):
            scale_lanes[which, half] = jnp.concatenate(
                [
                    kv_scales[half * rows_half + r, which]
                    for r in range(rows_half)
                ],
                axis=1,
            ) * (score_scale if which == 0 else 1.0)
    shape = (rows_half * group, HD)
    row_of = lax.broadcasted_iota(jnp.int32, shape, 0) >> (group.bit_length() - 1)
    lane = lax.broadcasted_iota(jnp.int32, shape, 1)
    slot = me * block_len + (lane & (block_len - 1))
    lane_row = lane >> (block_len.bit_length() - 1)
    masks = []
    for half in range(halves):
        live = jnp.zeros(shape, jnp.int32)
        for r in range(rows_half):
            live = jnp.where(row_of == r, lengths[half * rows_half + r], live)
        masks.append(
            jnp.where(
                (row_of == lane_row) & (slot < live), 0.0, NEG_FILL
            ).astype(f32)
        )

    kv_copy.wait()

    def attend(g, stats):
        lanes = pl.ds(pl.multiple_of(g * HD, HD), HD)
        result = []
        for half in range(halves):
            first = half * rows_half
            keys = kv_here[first : first + rows_half, 0, :, lanes].reshape(HD, HD)
            values = kv_here[first : first + rows_half, 1, :, lanes].reshape(HD, HD)
            query = q_all[g, half * shape[0] : (half + 1) * shape[0], :]
            raw = lax.dot_general(
                query, keys, (((1,), (1,)), ((), ())), preferred_element_type=f32
            )
            scores = raw * scale_lanes[0, half, pl.ds(g, 1), :] + masks[half]
            peak = jnp.maximum(jnp.max(scores, axis=1, keepdims=True), PEAK_FLOOR)
            weights = jnp.exp(scores - peak)
            total = jnp.sum(weights, axis=1, keepdims=True)
            weighted = weights * scale_lanes[1, half, pl.ds(g, 1), :]
            summed = jnp.dot(
                weighted.astype(jnp.bfloat16), values, preferred_element_type=f32
            ).astype(jnp.bfloat16)
            part_out[first : first + rows_half, g] = summed.reshape(
                rows_half, group, HD
            )
            stat = stats[half]
            stat = jnp.where(lane == g, peak, stat)
            result.append(jnp.where(lane == g + n, total, stat))
        return tuple(result)

    def part_copy(step, first=0, count=n):
        return pltpu.make_async_remote_copy(
            src_ref=part_out.at[peer_of(step), pl.ds(first, count)],
            dst_ref=part_in.at[me, pl.ds(first, count)],
            send_sem=part_send,
            recv_sem=part_recv,
            device_id=to(peer_of(step), core),
            device_id_type=DEVICE,
        )

    def stat_copy(step):
        return pltpu.make_async_remote_copy(
            src_ref=stat_out.at[peer_of(step)],
            dst_ref=stat_in.at[me],
            send_sem=stat_send,
            recv_sem=stat_recv,
            device_id=to(peer_of(step), core),
            device_id_type=DEVICE,
        )

    def arrivals(buffer, send, recv):
        return pltpu.make_async_remote_copy(
            src_ref=buffer.at[pl.ds(0, n - 1)],
            dst_ref=buffer.at[pl.ds(0, n - 1)],
            send_sem=send,
            recv_sem=recv,
            device_id=to(peer_of(1), core),
            device_id_type=DEVICE,
        )

    def send_part(step):
        first = peer_of(step) // 2 * 2
        for s in reversed(range(1, n)):
            part_copy(s, first, 2).start()

    def await_q(step):
        q_arrival(peer_of(step)).wait_recv()

    stats = attend(me, tuple(jnp.zeros(shape, f32) for _ in range(halves)))
    for step in range(1, n, 2):
        if step + 1 < n:
            await_q(step + 1)
            q_forward(step + 1).start()
        await_q(step)
        stats = attend(peer_of(step), stats)
        if step + 1 < n:
            stats = attend(peer_of(step + 1), stats)
        else:
            for half in range(halves):
                for r in range(rows_half):
                    upper = stats[half][r * group : r * group + group // 2]
                    lower = stats[half][r * group + group // 2 : (r + 1) * group]
                    stat_out[half * rows_half + r] = upper + pltpu.roll(lower, 2 * n, 1)
            for s in reversed(range(1, n)):
                stat_copy(s).start()
        send_part(step)
        if n - 2 - step >= 1:
            wo_copy(peer_of(n - 2 - step)).start()
        if n - 3 - step >= 0:
            wo_copy(peer_of(n - 3 - step)).start()
    part_in[me] = part_out[me]
    stat_in[me] = stat_out[me]

    fresh_pair = new_kv[me].astype(f32)
    angle_me = positions[me].astype(f32) * rates[...]
    cosine_me = jnp.cos(angle_me)
    sine_me = jnp.sin(angle_me) * sign
    fresh_keys = [
        turn(
            jnp.broadcast_to(fresh_pair[0:1, g * HD : (g + 1) * HD], (8, HD)),
            cosine_me,
            sine_me,
        )[0:1].astype(jnp.bfloat16).astype(f32)
        for g in range(n)
    ]
    fresh_values = [fresh_pair[1:2, g * HD : (g + 1) * HD] for g in range(n)]

    common = lax.broadcasted_iota(jnp.int32, (H, H), 0) & lax.broadcasted_iota(
        jnp.int32, (H, H), 1
    )
    parity = jnp.zeros((H, H), jnp.int32)
    for b in range(H.bit_length() - 1):
        parity = parity ^ (lax.shift_right_logical(common, b) & 1)
    sylvester = jnp.where(parity == 0, 1.0, -1.0).astype(jnp.bfloat16)

    order = permutation(group, 2 * n_rows)
    lane_g = lax.broadcasted_iota(jnp.int32, (group, HD), 1)
    fresh = jnp.zeros((group, HD), f32)
    own_rows = pl.ds(pl.multiple_of(me * group, group), group)
    for g in range(n):
        score = jnp.sum(
            q_all[g, own_rows, :].astype(f32) * fresh_keys[g], axis=1, keepdims=True
        )
        fresh = jnp.where(lane_g == g, score * score_scale, fresh)

    arrivals(stat_in, stat_send, stat_recv).wait_recv()
    stat = []
    for s in range(n):
        packed = stat_in[s]
        stat.append(
            jnp.concatenate([packed, pltpu.roll(packed, HD - 2 * n, 1)], axis=0)
        )
    top = fresh
    for s in range(n):
        top = jnp.maximum(top, stat[s])
    factor = [jnp.exp(stat[s] - top) for s in range(n)]
    fresh_factor = jnp.exp(fresh - top)
    total = fresh_factor
    for s in range(n):
        total = total + factor[s] * pltpu.roll(stat[s], HD - n, 1)
    inverse = 1.0 / total
    factor = [f * inverse for f in factor]
    fresh_factor = fresh_factor * inverse

    arrivals(part_in, part_send, part_recv).wait_recv()
    attended = []
    for g in range(n):
        mixed = fresh_factor[:, g : g + 1] * fresh_values[g]
        for s in range(n):
            mixed = mixed + factor[s][:, g : g + 1] * part_in[s, g].astype(f32)
        attended.append(mixed)
    attended = jnp.concatenate(attended, axis=0).astype(jnp.bfloat16)
    rotated = jnp.dot(sylvester, attended, preferred_element_type=f32) * (H ** (-0.5))
    rot_out[...] = rotated.astype(jnp.bfloat16).reshape(n, group, HD)

    def rot_copy(step, other):
        peer = peer_of(step)
        return pltpu.make_async_remote_copy(
            src_ref=rot_out.at[peer],
            dst_ref=rot_in.at[core, me],
            send_sem=rot_send.at[other],
            recv_sem=rot_recv.at[core],
            device_id=to(peer, side_of(other)),
            device_id_type=DEVICE,
        )

    def rot_arrival(other):
        side = side_of(other)
        count = pl.ds(0, n - 1 + other)
        return pltpu.make_async_remote_copy(
            src_ref=rot_out.at[count],
            dst_ref=rot_in.at[side, count],
            send_sem=rot_send.at[other],
            recv_sem=rot_recv.at[side],
            device_id=to(peer_of(1), side),
            device_id_type=DEVICE,
        )

    pairs = [(s, o) for s in reversed(range(n)) for o in range(2) if s or o]
    for step, other in pairs:
        rot_copy(step, other).start()
    rot_in[core, me] = rot_out[me]
    for other in range(2):
        rot_arrival(other).wait_recv()
    tiles = jnp.dot(
        order, rot_in[...].reshape(2 * n_rows * group, HD), preferred_element_type=f32
    ).astype(jnp.bfloat16)
    flat_rows = jnp.concatenate(
        [tiles[k * 2 * n_rows : (k + 1) * 2 * n_rows] for k in range(group)], axis=1
    )

    def share_copy(i, other):
        side = side_of(other)
        return pltpu.make_async_remote_copy(
            src_ref=share_out.at[side, i],
            dst_ref=share_in.at[core, me],
            send_sem=share_send.at[other],
            recv_sem=share_recv.at[core],
            device_id=to(i, side),
            device_id_type=DEVICE,
        )

    def share_arrival(other):
        side = side_of(other)
        count = pl.ds(0, n - 1 + other)
        return pltpu.make_async_remote_copy(
            src_ref=share_out.at[side, count],
            dst_ref=share_in.at[side, count],
            send_sem=share_send.at[other],
            recv_sem=share_recv.at[side],
            device_id=to(peer_of(1), side),
            device_id_type=DEVICE,
        )

    def project(i):
        wo_copy(i).wait()
        share = jnp.dot(flat_rows, wo_here[i], preferred_element_type=f32)
        for side in range(2):
            rows = share[side * n_rows : (side + 1) * n_rows]
            share_out[side, i] = jnp.concatenate(
                [rows[:, :half_wide], rows[:, half_wide:]], axis=0
            ).astype(jnp.bfloat16)

    def project_step(step, carry):
        i = peer_at(n - step)
        project(i)
        share_copy(i, 0).start()
        share_copy(i, 1).start()
        return carry

    lax.fori_loop(1, n, project_step, 0)
    project(me)
    share_copy(me, 1).start()
    share_in[core, me] = share_out[core, me]

    for other in range(2):
        share_arrival(other).wait_recv()
    for side in range(2):
        added = share_in[side, 0].astype(f32)
        for s in range(1, n):
            added = added + share_in[side, s].astype(f32)
        for half in range(2):
            first = side * wide + half * half_wide
            out[:, first : first + half_wide] = added[half * n_rows : (half + 1) * n_rows]

    for step in direct:
        q_copy(step).wait_send()
    for step in direct[1:]:
        q_forward(step).wait_send()
    arrivals(stat_out, stat_send, stat_recv).wait_send()
    arrivals(part_out, part_send, part_recv).wait_send()
    for other in range(2):
        rot_arrival(other).wait_send()
        share_arrival(other).wait_send()


def on_device_fused(
    queries, new_kv, positions, lengths, kv_codes, kv_scales, wo_codes, wo_scales, residual
):
    n = lax.axis_size("head")
    n_rows = queries.shape[0]
    group = queries.shape[1] // HD
    block_len = kv_codes.shape[2]
    width = wo_codes.shape[1]
    wide = width // n // 2
    halves = n_rows * block_len // HD
    rates = ROPE_BASE ** (-np.arange(HD // 2) * (2.0 / HD))
    rates = np.tile(rates, 2)[None, :].astype(np.float32)
    bf16, f32 = jnp.bfloat16, jnp.float32
    vmem = pl.BlockSpec(memory_space=pltpu.VMEM)
    hbm = pl.BlockSpec(memory_space=pltpu.HBM)
    dma = pltpu.SemaphoreType.DMA
    shares = pl.pallas_call(
        functools.partial(fused_kernel, n),
        out_shape=jax.ShapeDtypeStruct(residual.shape, f32),
        in_specs=[hbm] * 8,
        out_specs=vmem,
        scratch_shapes=[
            pltpu.SMEM(positions.shape, jnp.int32),
            pltpu.SMEM(lengths.shape, jnp.int32),
            pltpu.VMEM(rates.shape, f32),
            pltpu.VMEM(queries.shape, bf16),
            pltpu.VMEM(new_kv.shape, bf16),
            pltpu.VMEM(kv_scales.shape, f32),
            dma((6,)),
            pltpu.VMEM((n, n_rows * group, HD), bf16),
            pltpu.VMEM(kv_codes.shape, bf16),
            pltpu.VMEM((2, halves, KVH, HD), f32),
            pltpu.VMEM((n, n, group, HD), bf16),
            pltpu.VMEM((n, n, group, HD), bf16),
            pltpu.VMEM((n, group // 2, HD), f32),
            pltpu.VMEM((n, group // 2, HD), f32),
            pltpu.VMEM((n, group, HD), bf16),
            pltpu.VMEM((2, n, group, HD), bf16),
            pltpu.VMEM((n, wo_codes.shape[0], wide), bf16),
            pltpu.VMEM((2, n, 2 * n_rows, wide // 2), bf16),
            pltpu.VMEM((2, n, 2 * n_rows, wide // 2), bf16),
            dma,
            dma((n,)),
            dma((n + 1,)),
            dma((n,)),
            dma,
            dma,
            dma,
            dma,
            dma((2,)),
            dma((2,)),
            dma((2,)),
            dma((2,)),
        ],
        compiler_params=pltpu.CompilerParams(
            collective_id=0, has_side_effects=True, vmem_limit_bytes=64 * 1024 * 1024
        ),
        cost_estimate=pl.CostEstimate(
            flops=2 * 2 * n_rows * wo_codes.shape[0] * width // 2,
            bytes_accessed=wo_codes.shape[0] * width,
            transcendentals=0,
        ),
    )(
        positions,
        lengths,
        rates,
        queries,
        new_kv,
        kv_scales,
        kv_codes,
        wo_codes,
    )
    return (residual.astype(f32) + shares * wo_scales).astype(bf16)


def on_device(*arrays):
    queries, kv_codes, wo_codes = arrays[0], arrays[4], arrays[6]
    n = lax.axis_size("head")
    n_rows, group, block_len = queries.shape[0], queries.shape[1] // HD, kv_codes.shape[2]
    fits = (
        lax.axis_size("dp") == 2
        and n == KVH == n_rows
        and n & (n - 1) == 0
        and group == H // KVH == 16
        and block_len % 16 == 0
        and block_len < HD
        and HD % block_len == 0
        and n_rows * block_len % HD == 0
        and wo_codes.shape[1] % (n * 512) == 0
    )
    return (on_device_fused if fits else on_device_general)(*arrays)


def solution(mesh):
    placed = (
        P(("group", "dp"), "head"),
        P(("group", "dp"), None, None),
        P(("group", "dp")),
        P(("group", "dp")),
        P(("group", "dp"), None, "head", None),
        P(("group", "dp"), None, None, "head"),
        P("head", None),
        P("head"),
        P(("group", "dp"), "head"),
    )
    return jax.shard_map(
        on_device, mesh=mesh, in_specs=placed, out_specs=P(("group", "dp"), "head"), check_vma=False
    )
```

```python
import functools

import jax
import jax.numpy as jnp
import numpy as np
from jax import lax
from jax.experimental import pallas as pl
from jax.experimental.pallas import tpu as pltpu
from jax.sharding import PartitionSpec as P

H = 128
KVH = 8
HD = 128


ROPE_BASE = 500000.0
NEG_FILL = -1e30


def partner_2(block, axis, distance):
    count = lax.axis_size(axis)
    route = []
    for low in range(count):
        high = low | 1 << distance
        if high != low and high < count:
            route += [(low, high), (high, low)]
    return lax.ppermute(block, axis, route)


def rotary(values_in, positions):
    half_dim = values_in.shape[-1] // 2
    inverse_rate = ROPE_BASE ** (
        -(jnp.arange(half_dim, dtype=jnp.float32) * (2.0 / values_in.shape[-1]))
    )
    angles = positions.astype(jnp.float32)[:, None, None] * inverse_rate
    cosine = jnp.cos(angles)
    sine_part = jnp.sin(angles)
    lower_half = values_in[..., :half_dim]
    upper_half = values_in[..., half_dim:]
    return jnp.concatenate(
        [
            lower_half * cosine - upper_half * sine_part,
            upper_half * cosine + lower_half * sine_part,
        ],
        axis=-1,
    )


def hadamard(size_needed):
    index_row = jnp.arange(size_needed, dtype=jnp.int32)
    common = jnp.bitwise_and(index_row[:, None], index_row[None, :])
    parity = jnp.zeros_like(common)
    for bit_pos in range(max(size_needed.bit_length() - 1, 0)):
        parity = parity + jnp.right_shift(common, bit_pos) % 2
    return jnp.where(parity % 2 == 0, 1.0, -1.0).astype(jnp.float32)


def settle(peak_source, total_source, summed_source, fresh_score, fresh_values):
    peak_final = jnp.maximum(jnp.max(peak_source, axis=1), fresh_score)
    rescale = jnp.exp(peak_source - peak_final[:, None])
    fresh_weight = jnp.exp(fresh_score - peak_final)
    total_final = jnp.sum(total_source * rescale, axis=1) + fresh_weight
    summed_final = (
        jnp.sum(summed_source * rescale[..., None], axis=1) + fresh_weight[..., None] * fresh_values
    )
    return (summed_final / total_final[..., None]).astype(jnp.bfloat16)


def on_device_general(
    queries, new_kv, positions, lengths, kv_codes, kv_scales, wo_codes, wo_scales, residual
):
    n_head = lax.axis_size("head")
    my_index = lax.axis_index("head")
    n_rows = queries.shape[0]
    heads_here = queries.shape[1] // HD
    group_size = H // KVH
    block_len = kv_codes.shape[2]
    first_slot = my_index * block_len
    score_scale = HD ** (-0.5)
    own_query = rotary(
        queries.reshape(n_rows, heads_here, HD).astype(jnp.float32), positions
    ).astype(jnp.bfloat16)
    all_query = lax.all_gather(
        own_query.reshape(n_rows, heads_here * HD), "head", axis=1, tiled=True
    )
    all_query = all_query.reshape(n_rows, KVH, group_size, HD)
    fresh_keys = rotary(
        new_kv[:, 0].reshape(n_rows, KVH, HD).astype(jnp.float32), positions
    ).astype(jnp.bfloat16)
    fresh_values = new_kv[:, 1].reshape(n_rows, KVH, HD).astype(jnp.float32)
    key_codes = kv_codes[:, 0].reshape(n_rows, block_len, KVH, HD)
    value_codes = kv_codes[:, 1].reshape(n_rows, block_len, KVH, HD).astype(jnp.float32)
    raw_scores = jnp.einsum(
        "rgjd,rtgd->rgjt", all_query, key_codes, preferred_element_type=jnp.float32
    )
    scores = raw_scores * kv_scales[:, 0][:, :, None, :] * score_scale
    slot_index = first_slot + jnp.arange(block_len, dtype=jnp.int32)
    is_valid = (slot_index[None, :] < lengths[:, None])[:, None, None, :]
    scores = jnp.where(is_valid, scores, NEG_FILL)
    peak_here = jnp.max(scores, axis=-1)
    weights = jnp.where(is_valid, jnp.exp(scores - peak_here[..., None]), 0.0)
    total_here = jnp.sum(weights, axis=-1)
    summed = jnp.einsum(
        "rgjt,rtgd->rgjd",
        weights * kv_scales[:, 1][:, :, None, :],
        value_codes,
        precision=lax.Precision.HIGHEST,
    )
    peak_full = peak_here.reshape(n_rows, H)
    total_full = total_here.reshape(n_rows, H)
    summed_full = summed.reshape(n_rows, H, HD)
    received = (
        lax.all_to_all(peak_full, "head", split_axis=1, concat_axis=1, tiled=True),
        lax.all_to_all(total_full, "head", split_axis=1, concat_axis=1, tiled=True),
        lax.all_to_all(summed_full, "head", split_axis=1, concat_axis=1, tiled=True),
    )
    peak_source = received[0].reshape(n_rows, n_head, heads_here)
    total_source = received[1].reshape(n_rows, n_head, heads_here)
    summed_source = received[2].reshape(n_rows, n_head, heads_here, HD)
    owned_group = my_index * heads_here // group_size
    key_owned = lax.dynamic_index_in_dim(fresh_keys, owned_group, 1, keepdims=False)
    fresh_score = (
        jnp.einsum("rjd,rd->rj", own_query, key_owned, preferred_element_type=jnp.float32)
        * score_scale
    )
    value_owned = lax.dynamic_index_in_dim(fresh_values, owned_group, 1, keepdims=False)
    fresh_spread = jnp.broadcast_to(value_owned[:, None, :], (n_rows, heads_here, HD))
    attended = settle(peak_source, total_source, summed_source, fresh_score, fresh_spread)
    local_table = hadamard(heads_here)
    rotated = jnp.einsum(
        "kj,rjd->rkd", local_table, attended.astype(jnp.float32), precision=lax.Precision.HIGHEST
    )
    for bit_pos in range(n_head.bit_length() - 1):
        partner = partner_2(rotated, "head", bit_pos)
        is_upper = jnp.right_shift(my_index, bit_pos) % 2 == 1
        rotated = jnp.where(is_upper, partner - rotated, rotated + partner)
    flat_rows = (rotated * H ** (-0.5)).reshape(n_rows, heads_here * HD).astype(jnp.bfloat16)
    partial_out = jnp.dot(flat_rows, wo_codes, preferred_element_type=jnp.float32)
    shares = lax.psum_scatter(partial_out, "head", scatter_dimension=1, tiled=True)
    return (residual.astype(jnp.float32) + shares * wo_scales).astype(jnp.bfloat16)


PEAK_FLOOR = -1e29
DEVICE = pl.DeviceIdType.MESH


def fused_kernel(
    n,
    positions_far,
    lengths_far,
    rates_far,
    queries_far,
    new_kv_far,
    kv_scales_far,
    kv_codes,
    wo_codes,
    out,
    positions,
    lengths,
    rates,
    queries,
    new_kv,
    kv_scales,
    in_sem,
    q_all,
    kv_here,
    scale_lanes,
    part_out,
    part_in,
    stat_out,
    stat_in,
    rot_out,
    rot_in,
    wo_here,
    share_out,
    share_in,
    kv_sem,
    wo_sem,
    q_send,
    q_recv,
    part_send,
    part_recv,
    stat_send,
    stat_recv,
    rot_send,
    rot_recv,
    share_send,
    share_recv,
):
    me = lax.axis_index("head")
    core = lax.axis_index("dp")
    replica = lax.axis_index("group")
    quad = replica * 2 + core
    n_rows = queries.shape[0]
    group = queries.shape[1] // HD
    block_len = kv_codes.shape[2]
    wide = wo_here.shape[2]
    half_wide = wide // 2
    halves = n_rows * block_len // HD
    rows_half = n_rows // halves
    score_scale = HD ** (-0.5)
    f32 = jnp.float32

    n_bits = n.bit_length() - 1
    bits = [lax.rem(lax.div(me, 2**b), 2) for b in range(n_bits)]
    peers = [
        sum((1 - bits[b] if step >> b & 1 else bits[b]) * 2**b for b in range(n_bits))
        for step in range(n)
    ]
    other_core = 1 - core

    def peer_of(step):
        return peers[step]

    def peer_at(step):
        peer = 0
        for b in range(n_bits):
            bit = lax.rem(lax.div(step, 2**b), 2)
            peer += (bits[b] + bit - 2 * bits[b] * bit) * 2**b
        return peer

    def at(other):
        return (1 - replica if other >> 1 else replica, other_core if other & 1 else core)

    def quad_of(other):
        there, dp = at(other)
        return there * 2 + dp

    def to(head, dp):
        return {"group": replica, "head": head, "dp": dp}

    def to_quad(head, other):
        there, dp = at(other)
        return {"group": there, "head": head, "dp": dp}

    fetched = [
        pltpu.make_async_copy(far, near, in_sem.at[k])
        for k, (far, near) in enumerate(
            [
                (positions_far, positions),
                (rates_far, rates),
                (queries_far, queries),
                (lengths_far, lengths),
                (kv_scales_far, kv_scales),
                (new_kv_far, new_kv),
            ]
        )
    ]
    for copy in fetched:
        copy.start()
    kv_copy = pltpu.make_async_copy(kv_codes, kv_here, kv_sem)
    kv_copy.start()

    def wo_copy(i):
        first = pl.multiple_of((i * 4 + quad) * wide, wide)
        return pltpu.make_async_copy(
            wo_codes.at[:, pl.ds(first, wide)], wo_here.at[i], wo_sem.at[i]
        )

    barrier = pltpu.get_barrier_semaphore()
    for step in range(n):
        for other in range(4):
            if step or other:
                pl.semaphore_signal(
                    barrier,
                    inc=1,
                    device_id=to_quad(peer_of(step), other),
                    device_id_type=DEVICE,
                )

    lane_1 = lax.broadcasted_iota(jnp.int32, (1, HD), 1)
    row_8 = lax.broadcasted_iota(jnp.int32, (n_rows, HD), 0)
    for copy in fetched[:3]:
        copy.wait()
    pos = jnp.zeros((n_rows, HD), f32)
    for r in range(n_rows):
        pos = jnp.where(row_8 == r, positions[r].astype(f32), pos)
    sign = jnp.where(lane_1 < HD // 2, -1.0, 1.0).astype(f32)
    angle = pos * rates[...]
    cosine = jnp.cos(angle)
    sine = jnp.sin(angle) * sign

    def turn(v, c, s):
        return v * c + pltpu.roll(v, HD // 2, 1) * s

    stacked = jnp.concatenate(
        [
            turn(queries[:, j * HD : (j + 1) * HD].astype(f32), cosine, sine)
            for j in range(group)
        ],
        axis=0,
    ).astype(jnp.bfloat16)

    def permutation(major, minor):
        size = major * minor
        to_row = lax.broadcasted_iota(jnp.int32, (size, size), 0)
        from_row = lax.broadcasted_iota(jnp.int32, (size, size), 1)
        shift = minor.bit_length() - 1
        wanted = (to_row & (minor - 1)) * major + (to_row >> shift)
        return jnp.where(wanted == from_row, 1.0, 0.0).astype(jnp.bfloat16)

    q_all[me] = jnp.dot(
        permutation(n_rows, group), stacked, preferred_element_type=f32
    ).astype(jnp.bfloat16)

    pl.semaphore_wait(barrier, 4 * n - 1)

    def q_copy(step):
        return pltpu.make_async_remote_copy(
            src_ref=q_all.at[me],
            dst_ref=q_all.at[me],
            send_sem=q_send.at[step],
            recv_sem=q_recv.at[me],
            device_id=to(peer_of(step), core),
            device_id_type=DEVICE,
        )

    def q_forward(step):
        block = peer_of(step)
        return pltpu.make_async_remote_copy(
            src_ref=q_all.at[block],
            dst_ref=q_all.at[block],
            send_sem=q_send.at[step + 1],
            recv_sem=q_recv.at[block],
            device_id=to(peer_of(1), core),
            device_id_type=DEVICE,
        )

    def q_arrival(source):
        return pltpu.make_async_remote_copy(
            src_ref=q_all.at[source],
            dst_ref=q_all.at[source],
            send_sem=q_send.at[0],
            recv_sem=q_recv.at[source],
            device_id=to(source, core),
            device_id_type=DEVICE,
        )

    direct = [1] + list(range(2, n, 2))
    for step in direct:
        q_copy(step).start()
    for step in (n - 1, n - 2):
        wo_copy(peer_of(step)).start()
    for copy in fetched[3:]:
        copy.wait()

    for which in range(2):
        for half in range(halves):
            scale_lanes[which, half] = jnp.concatenate(
                [
                    kv_scales[half * rows_half + r, which]
                    for r in range(rows_half)
                ],
                axis=1,
            ) * (score_scale if which == 0 else 1.0)
    shape = (rows_half * group, HD)
    row_of = lax.broadcasted_iota(jnp.int32, shape, 0) >> (group.bit_length() - 1)
    lane = lax.broadcasted_iota(jnp.int32, shape, 1)
    slot = me * block_len + (lane & (block_len - 1))
    lane_row = lane >> (block_len.bit_length() - 1)
    masks = []
    for half in range(halves):
        live = jnp.zeros(shape, jnp.int32)
        for r in range(rows_half):
            live = jnp.where(row_of == r, lengths[half * rows_half + r], live)
        masks.append(
            jnp.where(
                (row_of == lane_row) & (slot < live), 0.0, NEG_FILL
            ).astype(f32)
        )

    kv_copy.wait()

    def attend(g, stats):
        lanes = pl.ds(pl.multiple_of(g * HD, HD), HD)
        result = []
        for half in range(halves):
            first = half * rows_half
            keys = kv_here[first : first + rows_half, 0, :, lanes].reshape(HD, HD)
            values = kv_here[first : first + rows_half, 1, :, lanes].reshape(HD, HD)
            query = q_all[g, half * shape[0] : (half + 1) * shape[0], :]
            raw = lax.dot_general(
                query, keys, (((1,), (1,)), ((), ())), preferred_element_type=f32
            )
            scores = raw * scale_lanes[0, half, pl.ds(g, 1), :] + masks[half]
            peak = jnp.maximum(jnp.max(scores, axis=1, keepdims=True), PEAK_FLOOR)
            weights = jnp.exp(scores - peak)
            total = jnp.sum(weights, axis=1, keepdims=True)
            weighted = weights * scale_lanes[1, half, pl.ds(g, 1), :]
            summed = jnp.dot(
                weighted.astype(jnp.bfloat16), values, preferred_element_type=f32
            ).astype(jnp.bfloat16)
            part_out[first : first + rows_half, g] = summed.reshape(
                rows_half, group, HD
            )
            stat = stats[half]
            stat = jnp.where(lane == g, peak, stat)
            result.append(jnp.where(lane == g + n, total, stat))
        return tuple(result)

    def part_copy(step, first=0, count=n):
        return pltpu.make_async_remote_copy(
            src_ref=part_out.at[peer_of(step), pl.ds(first, count)],
            dst_ref=part_in.at[me, pl.ds(first, count)],
            send_sem=part_send,
            recv_sem=part_recv,
            device_id=to(peer_of(step), core),
            device_id_type=DEVICE,
        )

    def stat_copy(step):
        return pltpu.make_async_remote_copy(
            src_ref=stat_out.at[peer_of(step)],
            dst_ref=stat_in.at[me],
            send_sem=stat_send,
            recv_sem=stat_recv,
            device_id=to(peer_of(step), core),
            device_id_type=DEVICE,
        )

    def arrivals(buffer, send, recv):
        return pltpu.make_async_remote_copy(
            src_ref=buffer.at[pl.ds(0, n - 1)],
            dst_ref=buffer.at[pl.ds(0, n - 1)],
            send_sem=send,
            recv_sem=recv,
            device_id=to(peer_of(1), core),
            device_id_type=DEVICE,
        )

    def send_part(step):
        first = peer_of(step) // 2 * 2
        for s in reversed(range(1, n)):
            part_copy(s, first, 2).start()

    def await_q(step):
        q_arrival(peer_of(step)).wait_recv()

    stats = attend(me, tuple(jnp.zeros(shape, f32) for _ in range(halves)))
    for step in range(1, n, 2):
        if step + 1 < n:
            await_q(step + 1)
            q_forward(step + 1).start()
        await_q(step)
        stats = attend(peer_of(step), stats)
        if step + 1 < n:
            stats = attend(peer_of(step + 1), stats)
        else:
            for half in range(halves):
                for r in range(rows_half):
                    upper = stats[half][r * group : r * group + group // 2]
                    lower = stats[half][r * group + group // 2 : (r + 1) * group]
                    stat_out[half * rows_half + r] = upper + pltpu.roll(lower, 2 * n, 1)
            for s in reversed(range(1, n)):
                stat_copy(s).start()
        send_part(step)
        if n - 2 - step >= 1:
            wo_copy(peer_of(n - 2 - step)).start()
        if n - 3 - step >= 0:
            wo_copy(peer_of(n - 3 - step)).start()
    part_in[me] = part_out[me]
    stat_in[me] = stat_out[me]

    fresh_pair = new_kv[me].astype(f32)
    angle_me = positions[me].astype(f32) * rates[...]
    cosine_me = jnp.cos(angle_me)
    sine_me = jnp.sin(angle_me) * sign
    fresh_keys = [
        turn(
            jnp.broadcast_to(fresh_pair[0:1, g * HD : (g + 1) * HD], (8, HD)),
            cosine_me,
            sine_me,
        )[0:1].astype(jnp.bfloat16).astype(f32)
        for g in range(n)
    ]
    fresh_values = [fresh_pair[1:2, g * HD : (g + 1) * HD] for g in range(n)]

    common = lax.broadcasted_iota(jnp.int32, (H, H), 0) & lax.broadcasted_iota(
        jnp.int32, (H, H), 1
    )
    parity = jnp.zeros((H, H), jnp.int32)
    for b in range(H.bit_length() - 1):
        parity = parity ^ (lax.shift_right_logical(common, b) & 1)
    sylvester = jnp.where(parity == 0, 1.0, -1.0).astype(jnp.bfloat16)

    order = permutation(group, n_rows)
    lane_g = lax.broadcasted_iota(jnp.int32, (group, HD), 1)
    fresh = jnp.zeros((group, HD), f32)
    own_rows = pl.ds(pl.multiple_of(me * group, group), group)
    for g in range(n):
        score = jnp.sum(
            q_all[g, own_rows, :].astype(f32) * fresh_keys[g], axis=1, keepdims=True
        )
        fresh = jnp.where(lane_g == g, score * score_scale, fresh)

    arrivals(stat_in, stat_send, stat_recv).wait_recv()
    stat = []
    for s in range(n):
        packed = stat_in[s]
        stat.append(
            jnp.concatenate([packed, pltpu.roll(packed, HD - 2 * n, 1)], axis=0)
        )
    top = fresh
    for s in range(n):
        top = jnp.maximum(top, stat[s])
    factor = [jnp.exp(stat[s] - top) for s in range(n)]
    fresh_factor = jnp.exp(fresh - top)
    total = fresh_factor
    for s in range(n):
        total = total + factor[s] * pltpu.roll(stat[s], HD - n, 1)
    inverse = 1.0 / total
    factor = [f * inverse for f in factor]
    fresh_factor = fresh_factor * inverse

    arrivals(part_in, part_send, part_recv).wait_recv()
    attended = []
    for g in range(n):
        mixed = fresh_factor[:, g : g + 1] * fresh_values[g]
        for s in range(n):
            mixed = mixed + factor[s][:, g : g + 1] * part_in[s, g].astype(f32)
        attended.append(mixed)
    attended = jnp.concatenate(attended, axis=0).astype(jnp.bfloat16)
    rotated = jnp.dot(sylvester, attended, preferred_element_type=f32) * (H ** (-0.5))
    rot_out[...] = rotated.astype(jnp.bfloat16).reshape(n, group, HD)

    def rot_copy(step, other):
        peer = peer_of(step)
        return pltpu.make_async_remote_copy(
            src_ref=rot_out.at[peer],
            dst_ref=rot_in.at[quad, me],
            send_sem=rot_send.at[other],
            recv_sem=rot_recv.at[quad],
            device_id=to_quad(peer, other),
            device_id_type=DEVICE,
        )

    def rot_arrival(other):
        count = pl.ds(0, n if other else n - 1)
        return pltpu.make_async_remote_copy(
            src_ref=rot_out.at[count],
            dst_ref=rot_in.at[quad_of(other), count],
            send_sem=rot_send.at[other],
            recv_sem=rot_recv.at[quad_of(other)],
            device_id=to_quad(peer_of(1), other),
            device_id_type=DEVICE,
        )

    pairs = [(s, o) for s in reversed(range(n)) for o in range(4) if s or o]
    for step, other in pairs:
        rot_copy(step, other).start()
    rot_in[quad, me] = rot_out[me]
    for other in range(4):
        rot_arrival(other).wait_recv()
    tiles = [
        jnp.dot(
            order, rot_in[q].reshape(n_rows * group, HD), preferred_element_type=f32
        )
        for q in range(4)
    ]
    flat_rows = jnp.concatenate(
        [
            jnp.concatenate([t[k * n_rows : (k + 1) * n_rows] for t in tiles], axis=0)
            for k in range(group)
        ],
        axis=1,
    ).astype(jnp.bfloat16)

    def share_copy(i, other):
        return pltpu.make_async_remote_copy(
            src_ref=share_out.at[quad_of(other), i],
            dst_ref=share_in.at[quad, me],
            send_sem=share_send.at[other],
            recv_sem=share_recv.at[quad],
            device_id=to_quad(i, other),
            device_id_type=DEVICE,
        )

    def share_arrival(other):
        count = pl.ds(0, n if other else n - 1)
        return pltpu.make_async_remote_copy(
            src_ref=share_out.at[quad_of(other), count],
            dst_ref=share_in.at[quad_of(other), count],
            send_sem=share_send.at[other],
            recv_sem=share_recv.at[quad_of(other)],
            device_id=to_quad(peer_of(1), other),
            device_id_type=DEVICE,
        )

    def project(i):
        wo_copy(i).wait()
        share = jnp.dot(flat_rows, wo_here[i], preferred_element_type=f32)
        for q in range(4):
            rows = share[q * n_rows : (q + 1) * n_rows]
            share_out[q, i] = jnp.concatenate(
                [rows[:, :half_wide], rows[:, half_wide:]], axis=0
            ).astype(jnp.bfloat16)

    def project_step(step, carry):
        i = peer_at(n - step)
        project(i)
        for other in range(4):
            share_copy(i, other).start()
        return carry

    lax.fori_loop(1, n, project_step, 0)
    project(me)
    for other in range(1, 4):
        share_copy(me, other).start()
    share_in[quad, me] = share_out[quad, me]

    for other in range(4):
        share_arrival(other).wait_recv()
    for q in range(4):
        added = share_in[q, 0].astype(f32)
        for s in range(1, n):
            added = added + share_in[q, s].astype(f32)
        for half in range(2):
            first = q * wide + half * half_wide
            out[:, first : first + half_wide] = added[half * n_rows : (half + 1) * n_rows]

    for step in direct:
        q_copy(step).wait_send()
    for step in direct[1:]:
        q_forward(step).wait_send()
    arrivals(stat_out, stat_send, stat_recv).wait_send()
    arrivals(part_out, part_send, part_recv).wait_send()
    for other in range(4):
        rot_arrival(other).wait_send()
        share_arrival(other).wait_send()


def on_device_fused(
    queries, new_kv, positions, lengths, kv_codes, kv_scales, wo_codes, wo_scales, residual
):
    n = lax.axis_size("head")
    n_rows = queries.shape[0]
    group = queries.shape[1] // HD
    block_len = kv_codes.shape[2]
    width = wo_codes.shape[1]
    wide = width // n // 4
    halves = n_rows * block_len // HD
    rates = ROPE_BASE ** (-np.arange(HD // 2) * (2.0 / HD))
    rates = np.tile(rates, 2)[None, :].astype(np.float32)
    bf16, f32 = jnp.bfloat16, jnp.float32
    vmem = pl.BlockSpec(memory_space=pltpu.VMEM)
    hbm = pl.BlockSpec(memory_space=pltpu.HBM)
    dma = pltpu.SemaphoreType.DMA
    shares = pl.pallas_call(
        functools.partial(fused_kernel, n),
        out_shape=jax.ShapeDtypeStruct(residual.shape, f32),
        in_specs=[hbm] * 8,
        out_specs=vmem,
        scratch_shapes=[
            pltpu.SMEM(positions.shape, jnp.int32),
            pltpu.SMEM(lengths.shape, jnp.int32),
            pltpu.VMEM(rates.shape, f32),
            pltpu.VMEM(queries.shape, bf16),
            pltpu.VMEM(new_kv.shape, bf16),
            pltpu.VMEM(kv_scales.shape, f32),
            dma((6,)),
            pltpu.VMEM((n, n_rows * group, HD), bf16),
            pltpu.VMEM(kv_codes.shape, bf16),
            pltpu.VMEM((2, halves, KVH, HD), f32),
            pltpu.VMEM((n, n, group, HD), bf16),
            pltpu.VMEM((n, n, group, HD), bf16),
            pltpu.VMEM((n, group // 2, HD), f32),
            pltpu.VMEM((n, group // 2, HD), f32),
            pltpu.VMEM((n, group, HD), bf16),
            pltpu.VMEM((4, n, group, HD), bf16),
            pltpu.VMEM((n, wo_codes.shape[0], wide), bf16),
            pltpu.VMEM((4, n, 2 * n_rows, wide // 2), bf16),
            pltpu.VMEM((4, n, 2 * n_rows, wide // 2), bf16),
            dma,
            dma((n,)),
            dma((n + 1,)),
            dma((n,)),
            dma,
            dma,
            dma,
            dma,
            dma((4,)),
            dma((4,)),
            dma((4,)),
            dma((4,)),
        ],
        compiler_params=pltpu.CompilerParams(
            collective_id=0, has_side_effects=True, vmem_limit_bytes=65408 * 1024
        ),
        cost_estimate=pl.CostEstimate(
            flops=2 * 2 * n_rows * wo_codes.shape[0] * width // 2,
            bytes_accessed=wo_codes.shape[0] * width,
            transcendentals=0,
        ),
    )(
        positions,
        lengths,
        rates,
        queries,
        new_kv,
        kv_scales,
        kv_codes,
        wo_codes,
    )
    return (residual.astype(f32) + shares * wo_scales).astype(bf16)


def on_device(*arrays):
    queries, kv_codes, wo_codes = arrays[0], arrays[4], arrays[6]
    n = lax.axis_size("head")
    n_rows, group, block_len = queries.shape[0], queries.shape[1] // HD, kv_codes.shape[2]
    fits = (
        lax.axis_size("dp") == 2
        and lax.axis_size("group") == 2
        and n == KVH == n_rows
        and n & (n - 1) == 0
        and group == H // KVH == 16
        and block_len % 16 == 0
        and block_len < HD
        and HD % block_len == 0
        and n_rows * block_len % HD == 0
        and wo_codes.shape[1] % (n * 1024) == 0
    )
    return (on_device_fused if fits else on_device_general)(*arrays)


def solution(mesh):
    placed = (
        P(("group", "dp"), "head"),
        P(("group", "dp"), None, None),
        P(("group", "dp")),
        P(("group", "dp")),
        P(("group", "dp"), None, "head", None),
        P(("group", "dp"), None, None, "head"),
        P("head", None),
        P("head"),
        P(("group", "dp"), "head"),
    )
    return jax.shard_map(
        on_device, mesh=mesh, in_specs=placed, out_specs=P(("group", "dp"), "head"), check_vma=False
    )
```

```python
import functools

import jax
import jax.numpy as jnp
import numpy as np
from jax import lax
from jax.experimental import pallas as pl
from jax.experimental.pallas import tpu as pltpu
from jax.sharding import PartitionSpec as P

H = 128
KVH = 8
HD = 128


ROPE_BASE = 500000.0
NEG_FILL = -1e30


def partner_2(block, axis, distance):
    count = lax.axis_size(axis)
    route = []
    for low in range(count):
        high = low | 1 << distance
        if high != low and high < count:
            route += [(low, high), (high, low)]
    return lax.ppermute(block, axis, route)


def rotary(values_in, positions):
    half_dim = values_in.shape[-1] // 2
    inverse_rate = ROPE_BASE ** (
        -(jnp.arange(half_dim, dtype=jnp.float32) * (2.0 / values_in.shape[-1]))
    )
    angles = positions.astype(jnp.float32)[:, None, None] * inverse_rate
    cosine = jnp.cos(angles)
    sine_part = jnp.sin(angles)
    lower_half = values_in[..., :half_dim]
    upper_half = values_in[..., half_dim:]
    return jnp.concatenate(
        [
            lower_half * cosine - upper_half * sine_part,
            upper_half * cosine + lower_half * sine_part,
        ],
        axis=-1,
    )


def hadamard(size_needed):
    index_row = jnp.arange(size_needed, dtype=jnp.int32)
    common = jnp.bitwise_and(index_row[:, None], index_row[None, :])
    parity = jnp.zeros_like(common)
    for bit_pos in range(max(size_needed.bit_length() - 1, 0)):
        parity = parity + jnp.right_shift(common, bit_pos) % 2
    return jnp.where(parity % 2 == 0, 1.0, -1.0).astype(jnp.float32)


def settle(peak_source, total_source, summed_source, fresh_score, fresh_values):
    peak_final = jnp.maximum(jnp.max(peak_source, axis=1), fresh_score)
    rescale = jnp.exp(peak_source - peak_final[:, None])
    fresh_weight = jnp.exp(fresh_score - peak_final)
    total_final = jnp.sum(total_source * rescale, axis=1) + fresh_weight
    summed_final = (
        jnp.sum(summed_source * rescale[..., None], axis=1) + fresh_weight[..., None] * fresh_values
    )
    return (summed_final / total_final[..., None]).astype(jnp.bfloat16)


def on_device_general(
    queries, new_kv, positions, lengths, kv_codes, kv_scales, wo_codes, wo_scales, residual
):
    n_head = lax.axis_size("head")
    my_index = lax.axis_index("head")
    n_rows = queries.shape[0]
    heads_here = queries.shape[1] // HD
    group_size = H // KVH
    block_len = kv_codes.shape[2]
    first_slot = my_index * block_len
    score_scale = HD ** (-0.5)
    own_query = rotary(
        queries.reshape(n_rows, heads_here, HD).astype(jnp.float32), positions
    ).astype(jnp.bfloat16)
    all_query = lax.all_gather(
        own_query.reshape(n_rows, heads_here * HD), "head", axis=1, tiled=True
    )
    all_query = all_query.reshape(n_rows, KVH, group_size, HD)
    fresh_keys = rotary(
        new_kv[:, 0].reshape(n_rows, KVH, HD).astype(jnp.float32), positions
    ).astype(jnp.bfloat16)
    fresh_values = new_kv[:, 1].reshape(n_rows, KVH, HD).astype(jnp.float32)
    key_codes = kv_codes[:, 0].reshape(n_rows, block_len, KVH, HD)
    value_codes = kv_codes[:, 1].reshape(n_rows, block_len, KVH, HD).astype(jnp.float32)
    raw_scores = jnp.einsum(
        "rgjd,rtgd->rgjt", all_query, key_codes, preferred_element_type=jnp.float32
    )
    scores = raw_scores * kv_scales[:, 0][:, :, None, :] * score_scale
    slot_index = first_slot + jnp.arange(block_len, dtype=jnp.int32)
    is_valid = (slot_index[None, :] < lengths[:, None])[:, None, None, :]
    scores = jnp.where(is_valid, scores, NEG_FILL)
    peak_here = jnp.max(scores, axis=-1)
    weights = jnp.where(is_valid, jnp.exp(scores - peak_here[..., None]), 0.0)
    total_here = jnp.sum(weights, axis=-1)
    summed = jnp.einsum(
        "rgjt,rtgd->rgjd",
        weights * kv_scales[:, 1][:, :, None, :],
        value_codes,
        precision=lax.Precision.HIGHEST,
    )
    peak_full = peak_here.reshape(n_rows, H)
    total_full = total_here.reshape(n_rows, H)
    summed_full = summed.reshape(n_rows, H, HD)
    received = (
        lax.all_to_all(peak_full, "head", split_axis=1, concat_axis=1, tiled=True),
        lax.all_to_all(total_full, "head", split_axis=1, concat_axis=1, tiled=True),
        lax.all_to_all(summed_full, "head", split_axis=1, concat_axis=1, tiled=True),
    )
    peak_source = received[0].reshape(n_rows, n_head, heads_here)
    total_source = received[1].reshape(n_rows, n_head, heads_here)
    summed_source = received[2].reshape(n_rows, n_head, heads_here, HD)
    owned_group = my_index * heads_here // group_size
    key_owned = lax.dynamic_index_in_dim(fresh_keys, owned_group, 1, keepdims=False)
    fresh_score = (
        jnp.einsum("rjd,rd->rj", own_query, key_owned, preferred_element_type=jnp.float32)
        * score_scale
    )
    value_owned = lax.dynamic_index_in_dim(fresh_values, owned_group, 1, keepdims=False)
    fresh_spread = jnp.broadcast_to(value_owned[:, None, :], (n_rows, heads_here, HD))
    attended = settle(peak_source, total_source, summed_source, fresh_score, fresh_spread)
    local_table = hadamard(heads_here)
    rotated = jnp.einsum(
        "kj,rjd->rkd", local_table, attended.astype(jnp.float32), precision=lax.Precision.HIGHEST
    )
    for bit_pos in range(n_head.bit_length() - 1):
        partner = partner_2(rotated, "head", bit_pos)
        is_upper = jnp.right_shift(my_index, bit_pos) % 2 == 1
        rotated = jnp.where(is_upper, partner - rotated, rotated + partner)
    flat_rows = (rotated * H ** (-0.5)).reshape(n_rows, heads_here * HD).astype(jnp.bfloat16)
    partial_out = jnp.dot(flat_rows, wo_codes, preferred_element_type=jnp.float32)
    shares = lax.psum_scatter(partial_out, "head", scatter_dimension=1, tiled=True)
    return (residual.astype(jnp.float32) + shares * wo_scales).astype(jnp.bfloat16)


PEAK_FLOOR = -1e29
DEVICE = pl.DeviceIdType.MESH


def fused_kernel(
    n,
    positions_far,
    lengths_far,
    rates_far,
    queries_far,
    new_kv_far,
    kv_scales_far,
    kv_codes,
    wo_codes,
    out,
    positions,
    lengths,
    rates,
    queries,
    new_kv,
    kv_scales,
    in_sem,
    q_all,
    kv_here,
    scale_lanes,
    part_out,
    part_in,
    rot_out,
    rot_in,
    wo_here,
    share_out,
    share_in,
    kv_sem,
    wo_sem,
    q_send,
    q_recv,
    part_send,
    part_recv,
    rot_send,
    rot_recv,
    share_send,
    share_recv,
):
    me = lax.axis_index("head")
    core = lax.axis_index("dp")
    replica = lax.axis_index("group")
    n_rows = queries.shape[0]
    group = queries.shape[1] // HD
    block_len = kv_codes.shape[2]
    wide = wo_here.shape[2]
    half_wide = wide // 2
    halves = n_rows * block_len // HD
    rows_half = n_rows // halves
    score_scale = HD ** (-0.5)
    f32 = jnp.float32

    n_bits = n.bit_length() - 1
    bits = [lax.rem(lax.div(me, 2**b), 2) for b in range(n_bits)]
    peers = [
        sum((1 - bits[b] if step >> b & 1 else bits[b]) * 2**b for b in range(n_bits))
        for step in range(n)
    ]
    other_core = 1 - core

    def peer_of(step):
        return peers[step]

    def peer_at(step):
        peer = 0
        for b in range(n_bits):
            bit = lax.rem(lax.div(step, 2**b), 2)
            peer += (bits[b] + bit - 2 * bits[b] * bit) * 2**b
        return peer

    def side_of(other):
        return other_core if other else core

    def to(head, dp):
        return {"group": replica, "head": head, "dp": dp}

    fetched = [
        pltpu.make_async_copy(far, near, in_sem.at[k])
        for k, (far, near) in enumerate(
            [
                (positions_far, positions),
                (rates_far, rates),
                (queries_far, queries),
                (lengths_far, lengths),
                (kv_scales_far, kv_scales),
                (new_kv_far, new_kv),
            ]
        )
    ]
    for copy in fetched:
        copy.start()
    kv_copy = pltpu.make_async_copy(kv_codes, kv_here, kv_sem)
    kv_copy.start()

    def wo_copy(i):
        first = pl.multiple_of(i * (2 * wide) + core * wide, wide)
        return pltpu.make_async_copy(
            wo_codes.at[:, pl.ds(first, wide)], wo_here.at[i], wo_sem.at[i]
        )

    barrier = pltpu.get_barrier_semaphore()
    for step in range(n):
        for other in range(2):
            if step or other:
                pl.semaphore_signal(
                    barrier,
                    inc=1,
                    device_id=to(peer_of(step), side_of(other)),
                    device_id_type=DEVICE,
                )

    lane_1 = lax.broadcasted_iota(jnp.int32, (1, HD), 1)
    row_8 = lax.broadcasted_iota(jnp.int32, (n_rows, HD), 0)
    for copy in fetched[:3]:
        copy.wait()
    pos = jnp.zeros((n_rows, HD), f32)
    for r in range(n_rows):
        pos = jnp.where(row_8 == r, positions[r].astype(f32), pos)
    sign = jnp.where(lane_1 < HD // 2, -1.0, 1.0).astype(f32)
    angle = pos * rates[...]
    cosine = jnp.cos(angle)
    sine = jnp.sin(angle) * sign

    def turn(v, c, s):
        return v * c + pltpu.roll(v, HD // 2, 1) * s

    stacked = jnp.concatenate(
        [
            turn(queries[:, j * HD : (j + 1) * HD].astype(f32), cosine, sine)
            for j in range(group)
        ],
        axis=0,
    ).astype(jnp.bfloat16)

    def permutation(major, minor):
        size = major * minor
        to_row = lax.broadcasted_iota(jnp.int32, (size, size), 0)
        from_row = lax.broadcasted_iota(jnp.int32, (size, size), 1)
        shift = minor.bit_length() - 1
        wanted = (to_row & (minor - 1)) * major + (to_row >> shift)
        return jnp.where(wanted == from_row, 1.0, 0.0).astype(jnp.bfloat16)

    q_all[me] = jnp.dot(
        permutation(n_rows, group), stacked, preferred_element_type=f32
    ).astype(jnp.bfloat16)

    pl.semaphore_wait(barrier, 2 * n - 1)

    def q_copy(step):
        return pltpu.make_async_remote_copy(
            src_ref=q_all.at[me],
            dst_ref=q_all.at[me],
            send_sem=q_send.at[step],
            recv_sem=q_recv.at[me],
            device_id=to(peer_of(step), core),
            device_id_type=DEVICE,
        )

    def q_forward(step):
        block = peer_of(step)
        return pltpu.make_async_remote_copy(
            src_ref=q_all.at[block],
            dst_ref=q_all.at[block],
            send_sem=q_send.at[step + 1],
            recv_sem=q_recv.at[block],
            device_id=to(peer_of(1), core),
            device_id_type=DEVICE,
        )

    def q_arrival(source):
        return pltpu.make_async_remote_copy(
            src_ref=q_all.at[source],
            dst_ref=q_all.at[source],
            send_sem=q_send.at[0],
            recv_sem=q_recv.at[source],
            device_id=to(source, core),
            device_id_type=DEVICE,
        )

    direct = [1] + list(range(2, n, 2))
    for step in direct:
        q_copy(step).start()
    for step in (n - 1, n - 2):
        wo_copy(peer_of(step)).start()
    for copy in fetched[3:]:
        copy.wait()

    for which in range(2):
        for half in range(halves):
            scale_lanes[which, half] = jnp.concatenate(
                [
                    kv_scales[half * rows_half + r, which]
                    for r in range(rows_half)
                ],
                axis=1,
            ) * (score_scale if which == 0 else 1.0)
    shape = (rows_half * group, HD)
    row_of = lax.broadcasted_iota(jnp.int32, shape, 0) >> (group.bit_length() - 1)
    lane = lax.broadcasted_iota(jnp.int32, shape, 1)
    slot = me * block_len + (lane & (block_len - 1))
    lane_row = lane >> (block_len.bit_length() - 1)
    masks = []
    for half in range(halves):
        live = jnp.zeros(shape, jnp.int32)
        for r in range(rows_half):
            live = jnp.where(row_of == r, lengths[half * rows_half + r], live)
        masks.append(
            jnp.where(
                (row_of == lane_row) & (slot < live), 0.0, NEG_FILL
            ).astype(f32)
        )

    kv_copy.wait()

    def attend(g, stats):
        lanes = pl.ds(pl.multiple_of(g * HD, HD), HD)
        result = []
        for half in range(halves):
            first = half * rows_half
            keys = kv_here[first : first + rows_half, 0, :, lanes].reshape(HD, HD)
            values = kv_here[first : first + rows_half, 1, :, lanes].reshape(HD, HD)
            query = q_all[g, half * shape[0] : (half + 1) * shape[0], :]
            raw = lax.dot_general(
                query, keys, (((1,), (1,)), ((), ())), preferred_element_type=f32
            )
            scores = raw * scale_lanes[0, half, pl.ds(g, 1), :] + masks[half]
            peak = jnp.maximum(jnp.max(scores, axis=1, keepdims=True), PEAK_FLOOR)
            weights = jnp.exp(scores - peak)
            total = jnp.sum(weights, axis=1, keepdims=True)
            weighted = weights * scale_lanes[1, half, pl.ds(g, 1), :]
            summed = jnp.dot(
                weighted.astype(jnp.bfloat16), values, preferred_element_type=f32
            ).astype(jnp.bfloat16)
            part_out[first : first + rows_half, g + 1] = summed.reshape(
                rows_half, group, HD
            )
            stat = stats[half]
            stat = jnp.where(lane == g, peak, stat)
            result.append(jnp.where(lane == g + n, total, stat))
        return tuple(result)

    block = lax.div(me, n // 2)

    def part_copy(step, first, count):
        return pltpu.make_async_remote_copy(
            src_ref=part_out.at[peer_of(step), pl.ds(first, count)],
            dst_ref=part_in.at[me, pl.ds(first, count)],
            send_sem=part_send,
            recv_sem=part_recv,
            device_id=to(peer_of(step), core),
            device_id_type=DEVICE,
        )

    def arrivals(buffer, send, recv):
        return pltpu.make_async_remote_copy(
            src_ref=buffer.at[pl.ds(0, n - 1), pl.ds(0, n + 1)],
            dst_ref=buffer.at[pl.ds(0, n - 1), pl.ds(0, n + 1)],
            send_sem=send,
            recv_sem=recv,
            device_id=to(peer_of(1), core),
            device_id_type=DEVICE,
        )

    def send_part(last):
        if last:
            first, count = (1 - block) * (n // 2 + 1), n // 2 + 1
        else:
            first, count = block * (n // 2) + 1, n // 2
        for s in reversed(range(1, n)):
            part_copy(s, first, count).start()

    def await_q(step):
        q_arrival(peer_of(step)).wait_recv()

    stats = attend(me, tuple(jnp.zeros(shape, f32) for _ in range(halves)))
    for step in range(1, n, 2):
        if step + 1 < n:
            await_q(step + 1)
            q_forward(step + 1).start()
        await_q(step)
        stats = attend(peer_of(step), stats)
        if step + 1 < n:
            stats = attend(peer_of(step + 1), stats)
        else:
            for half in range(halves):
                for r in range(rows_half):
                    exact = stats[half][r * group : (r + 1) * group]
                    packed = jnp.zeros((group, HD), f32)
                    for piece in range(3):
                        rounded = exact.astype(jnp.bfloat16).astype(f32)
                        exact = exact - rounded
                        if piece:
                            rounded = pltpu.roll(rounded, piece * 2 * n, 1)
                        packed = packed + rounded
                    packed = packed.astype(jnp.bfloat16)
                    part_out[half * rows_half + r, 0] = packed
                    part_out[half * rows_half + r, n + 1] = packed
            send_part(True)
        if step == n // 2 - 1:
            send_part(False)
        if n - 2 - step >= 1:
            wo_copy(peer_of(n - 2 - step)).start()
        if n - 3 - step >= 0:
            wo_copy(peer_of(n - 3 - step)).start()
    part_in[me] = part_out[me]

    fresh_pair = new_kv[me].astype(f32)
    angle_me = positions[me].astype(f32) * rates[...]
    cosine_me = jnp.cos(angle_me)
    sine_me = jnp.sin(angle_me) * sign
    fresh_keys = [
        turn(
            jnp.broadcast_to(fresh_pair[0:1, g * HD : (g + 1) * HD], (8, HD)),
            cosine_me,
            sine_me,
        )[0:1].astype(jnp.bfloat16).astype(f32)
        for g in range(n)
    ]
    fresh_values = [fresh_pair[1:2, g * HD : (g + 1) * HD] for g in range(n)]

    common = lax.broadcasted_iota(jnp.int32, (H, H), 0) & lax.broadcasted_iota(
        jnp.int32, (H, H), 1
    )
    parity = jnp.zeros((H, H), jnp.int32)
    for b in range(H.bit_length() - 1):
        parity = parity ^ (lax.shift_right_logical(common, b) & 1)
    sylvester = jnp.where(parity == 0, 1.0, -1.0).astype(jnp.bfloat16)

    order = permutation(group, 2 * n_rows)
    lane_g = lax.broadcasted_iota(jnp.int32, (group, HD), 1)
    fresh = jnp.zeros((group, HD), f32)
    own_rows = pl.ds(pl.multiple_of(me * group, group), group)
    for g in range(n):
        score = jnp.sum(
            q_all[g, own_rows, :].astype(f32) * fresh_keys[g], axis=1, keepdims=True
        )
        fresh = jnp.where(lane_g == g, score * score_scale, fresh)

    arrivals(part_in, part_send, part_recv).wait_recv()
    stat = []
    for s in range(n):
        packed = part_in[s, n + 1 if s < n // 2 else 0].astype(f32)
        stat.append(
            packed
            + pltpu.roll(packed, HD - 2 * n, 1)
            + pltpu.roll(packed, HD - 4 * n, 1)
        )
    top = fresh
    for s in range(n):
        top = jnp.maximum(top, stat[s])
    factor = [jnp.exp(stat[s] - top) for s in range(n)]
    fresh_factor = jnp.exp(fresh - top)
    total = fresh_factor
    for s in range(n):
        total = total + factor[s] * pltpu.roll(stat[s], HD - n, 1)
    inverse = 1.0 / total
    factor = [f * inverse for f in factor]
    fresh_factor = fresh_factor * inverse

    attended = []
    for g in range(n):
        mixed = fresh_factor[:, g : g + 1] * fresh_values[g]
        for s in range(n):
            mixed = mixed + factor[s][:, g : g + 1] * part_in[s, g + 1].astype(f32)
        attended.append(mixed)
    attended = jnp.concatenate(attended, axis=0).astype(jnp.bfloat16)
    rotated = jnp.dot(sylvester, attended, preferred_element_type=f32) * (H ** (-0.5))
    rot_out[...] = rotated.astype(jnp.bfloat16).reshape(n, group, HD)

    def rot_copy(step, other):
        peer = peer_of(step)
        return pltpu.make_async_remote_copy(
            src_ref=rot_out.at[peer],
            dst_ref=rot_in.at[core, me],
            send_sem=rot_send.at[other],
            recv_sem=rot_recv.at[core],
            device_id=to(peer, side_of(other)),
            device_id_type=DEVICE,
        )

    def rot_arrival(other):
        side = side_of(other)
        count = pl.ds(0, n - 1 + other)
        return pltpu.make_async_remote_copy(
            src_ref=rot_out.at[count],
            dst_ref=rot_in.at[side, count],
            send_sem=rot_send.at[other],
            recv_sem=rot_recv.at[side],
            device_id=to(peer_of(1), side),
            device_id_type=DEVICE,
        )

    pairs = [(s, o) for s in reversed(range(n)) for o in range(2) if s or o]
    for step, other in pairs:
        rot_copy(step, other).start()
    rot_in[core, me] = rot_out[me]
    for other in range(2):
        rot_arrival(other).wait_recv()
    tiles = jnp.dot(
        order, rot_in[...].reshape(2 * n_rows * group, HD), preferred_element_type=f32
    ).astype(jnp.bfloat16)
    flat_rows = jnp.concatenate(
        [tiles[k * 2 * n_rows : (k + 1) * 2 * n_rows] for k in range(group)], axis=1
    )

    def share_copy(i, other):
        side = side_of(other)
        return pltpu.make_async_remote_copy(
            src_ref=share_out.at[side, i],
            dst_ref=share_in.at[core, me],
            send_sem=share_send.at[other],
            recv_sem=share_recv.at[core],
            device_id=to(i, side),
            device_id_type=DEVICE,
        )

    def share_arrival(other):
        side = side_of(other)
        count = pl.ds(0, n - 1 + other)
        return pltpu.make_async_remote_copy(
            src_ref=share_out.at[side, count],
            dst_ref=share_in.at[side, count],
            send_sem=share_send.at[other],
            recv_sem=share_recv.at[side],
            device_id=to(peer_of(1), side),
            device_id_type=DEVICE,
        )

    def project(i):
        wo_copy(i).wait()
        share = jnp.dot(flat_rows, wo_here[i], preferred_element_type=f32)
        for side in range(2):
            rows = share[side * n_rows : (side + 1) * n_rows]
            share_out[side, i] = jnp.concatenate(
                [rows[:, :half_wide], rows[:, half_wide:]], axis=0
            ).astype(jnp.bfloat16)

    def project_step(step, carry):
        i = peer_at(n - step)
        project(i)
        share_copy(i, 0).start()
        share_copy(i, 1).start()
        return carry

    lax.fori_loop(1, n, project_step, 0)
    project(me)
    share_copy(me, 1).start()
    share_in[core, me] = share_out[core, me]

    for other in range(2):
        share_arrival(other).wait_recv()
    for side in range(2):
        added = share_in[side, 0].astype(f32)
        for s in range(1, n):
            added = added + share_in[side, s].astype(f32)
        for half in range(2):
            first = side * wide + half * half_wide
            out[:, first : first + half_wide] = added[half * n_rows : (half + 1) * n_rows]

    for step in direct:
        q_copy(step).wait_send()
    for step in direct[1:]:
        q_forward(step).wait_send()
    arrivals(part_out, part_send, part_recv).wait_send()
    for other in range(2):
        rot_arrival(other).wait_send()
        share_arrival(other).wait_send()


def on_device_fused(
    queries, new_kv, positions, lengths, kv_codes, kv_scales, wo_codes, wo_scales, residual
):
    n = lax.axis_size("head")
    n_rows = queries.shape[0]
    group = queries.shape[1] // HD
    block_len = kv_codes.shape[2]
    width = wo_codes.shape[1]
    wide = width // n // 2
    halves = n_rows * block_len // HD
    rates = ROPE_BASE ** (-np.arange(HD // 2) * (2.0 / HD))
    rates = np.tile(rates, 2)[None, :].astype(np.float32)
    bf16, f32 = jnp.bfloat16, jnp.float32
    vmem = pl.BlockSpec(memory_space=pltpu.VMEM)
    hbm = pl.BlockSpec(memory_space=pltpu.HBM)
    dma = pltpu.SemaphoreType.DMA
    shares = pl.pallas_call(
        functools.partial(fused_kernel, n),
        out_shape=jax.ShapeDtypeStruct(residual.shape, f32),
        in_specs=[hbm] * 8,
        out_specs=vmem,
        scratch_shapes=[
            pltpu.SMEM(positions.shape, jnp.int32),
            pltpu.SMEM(lengths.shape, jnp.int32),
            pltpu.VMEM(rates.shape, f32),
            pltpu.VMEM(queries.shape, bf16),
            pltpu.VMEM(new_kv.shape, bf16),
            pltpu.VMEM(kv_scales.shape, f32),
            dma((6,)),
            pltpu.VMEM((n, n_rows * group, HD), bf16),
            pltpu.VMEM(kv_codes.shape, bf16),
            pltpu.VMEM((2, halves, KVH, HD), f32),
            pltpu.VMEM((n, n + 2, group, HD), bf16),
            pltpu.VMEM((n, n + 2, group, HD), bf16),
            pltpu.VMEM((n, group, HD), bf16),
            pltpu.VMEM((2, n, group, HD), bf16),
            pltpu.VMEM((n, wo_codes.shape[0], wide), bf16),
            pltpu.VMEM((2, n, 2 * n_rows, wide // 2), bf16),
            pltpu.VMEM((2, n, 2 * n_rows, wide // 2), bf16),
            dma,
            dma((n,)),
            dma((n + 1,)),
            dma((n,)),
            dma,
            dma,
            dma((2,)),
            dma((2,)),
            dma((2,)),
            dma((2,)),
        ],
        compiler_params=pltpu.CompilerParams(
            collective_id=0, has_side_effects=True, vmem_limit_bytes=64 * 1024 * 1024
        ),
        cost_estimate=pl.CostEstimate(
            flops=2 * 2 * n_rows * wo_codes.shape[0] * width // 2,
            bytes_accessed=wo_codes.shape[0] * width,
            transcendentals=0,
        ),
    )(
        positions,
        lengths,
        rates,
        queries,
        new_kv,
        kv_scales,
        kv_codes,
        wo_codes,
    )
    return (residual.astype(f32) + shares * wo_scales).astype(bf16)


def on_device(*arrays):
    queries, kv_codes, wo_codes = arrays[0], arrays[4], arrays[6]
    n = lax.axis_size("head")
    n_rows, group, block_len = queries.shape[0], queries.shape[1] // HD, kv_codes.shape[2]
    fits = (
        lax.axis_size("dp") == 2
        and n == KVH == n_rows
        and n & (n - 1) == 0
        and group == H // KVH == 16
        and block_len % 16 == 0
        and block_len < HD
        and HD % block_len == 0
        and n_rows * block_len % HD == 0
        and wo_codes.shape[1] % (n * 512) == 0
    )
    return (on_device_fused if fits else on_device_general)(*arrays)


def solution(mesh):
    placed = (
        P(("group", "dp"), "head"),
        P(("group", "dp"), None, None),
        P(("group", "dp")),
        P(("group", "dp")),
        P(("group", "dp"), None, "head", None),
        P(("group", "dp"), None, None, "head"),
        P("head", None),
        P("head"),
        P(("group", "dp"), "head"),
    )
    return jax.shard_map(
        on_device, mesh=mesh, in_specs=placed, out_specs=P(("group", "dp"), "head"), check_vma=False
    )
```

```python
import functools

import jax
import jax.numpy as jnp
import numpy as np
from jax import lax
from jax.experimental import pallas as pl
from jax.experimental.pallas import tpu as pltpu
from jax.sharding import PartitionSpec as P

H = 128
KVH = 8
HD = 128


ROPE_BASE = 500000.0
NEG_FILL = -1e30


def partner_2(block, axis, distance):
    count = lax.axis_size(axis)
    route = []
    for low in range(count):
        high = low | 1 << distance
        if high != low and high < count:
            route += [(low, high), (high, low)]
    return lax.ppermute(block, axis, route)


def rotary(values_in, positions):
    half_dim = values_in.shape[-1] // 2
    inverse_rate = ROPE_BASE ** (
        -(jnp.arange(half_dim, dtype=jnp.float32) * (2.0 / values_in.shape[-1]))
    )
    angles = positions.astype(jnp.float32)[:, None, None] * inverse_rate
    cosine = jnp.cos(angles)
    sine_part = jnp.sin(angles)
    lower_half = values_in[..., :half_dim]
    upper_half = values_in[..., half_dim:]
    return jnp.concatenate(
        [
            lower_half * cosine - upper_half * sine_part,
            upper_half * cosine + lower_half * sine_part,
        ],
        axis=-1,
    )


def hadamard(size_needed):
    index_row = jnp.arange(size_needed, dtype=jnp.int32)
    common = jnp.bitwise_and(index_row[:, None], index_row[None, :])
    parity = jnp.zeros_like(common)
    for bit_pos in range(max(size_needed.bit_length() - 1, 0)):
        parity = parity + jnp.right_shift(common, bit_pos) % 2
    return jnp.where(parity % 2 == 0, 1.0, -1.0).astype(jnp.float32)


def settle(peak_source, total_source, summed_source, fresh_score, fresh_values):
    peak_final = jnp.maximum(jnp.max(peak_source, axis=1), fresh_score)
    rescale = jnp.exp(peak_source - peak_final[:, None])
    fresh_weight = jnp.exp(fresh_score - peak_final)
    total_final = jnp.sum(total_source * rescale, axis=1) + fresh_weight
    summed_final = (
        jnp.sum(summed_source * rescale[..., None], axis=1) + fresh_weight[..., None] * fresh_values
    )
    return (summed_final / total_final[..., None]).astype(jnp.bfloat16)


def on_device_general(
    queries, new_kv, positions, lengths, kv_codes, kv_scales, wo_codes, wo_scales, residual
):
    n_head = lax.axis_size("head")
    my_index = lax.axis_index("head")
    n_rows = queries.shape[0]
    heads_here = queries.shape[1] // HD
    group_size = H // KVH
    block_len = kv_codes.shape[2]
    first_slot = my_index * block_len
    score_scale = HD ** (-0.5)
    own_query = rotary(
        queries.reshape(n_rows, heads_here, HD).astype(jnp.float32), positions
    ).astype(jnp.bfloat16)
    all_query = lax.all_gather(
        own_query.reshape(n_rows, heads_here * HD), "head", axis=1, tiled=True
    )
    all_query = all_query.reshape(n_rows, KVH, group_size, HD)
    fresh_keys = rotary(
        new_kv[:, 0].reshape(n_rows, KVH, HD).astype(jnp.float32), positions
    ).astype(jnp.bfloat16)
    fresh_values = new_kv[:, 1].reshape(n_rows, KVH, HD).astype(jnp.float32)
    key_codes = kv_codes[:, 0].reshape(n_rows, block_len, KVH, HD)
    value_codes = kv_codes[:, 1].reshape(n_rows, block_len, KVH, HD).astype(jnp.float32)
    raw_scores = jnp.einsum(
        "rgjd,rtgd->rgjt", all_query, key_codes, preferred_element_type=jnp.float32
    )
    scores = raw_scores * kv_scales[:, 0][:, :, None, :] * score_scale
    slot_index = first_slot + jnp.arange(block_len, dtype=jnp.int32)
    is_valid = (slot_index[None, :] < lengths[:, None])[:, None, None, :]
    scores = jnp.where(is_valid, scores, NEG_FILL)
    peak_here = jnp.max(scores, axis=-1)
    weights = jnp.where(is_valid, jnp.exp(scores - peak_here[..., None]), 0.0)
    total_here = jnp.sum(weights, axis=-1)
    summed = jnp.einsum(
        "rgjt,rtgd->rgjd",
        weights * kv_scales[:, 1][:, :, None, :],
        value_codes,
        precision=lax.Precision.HIGHEST,
    )
    peak_full = peak_here.reshape(n_rows, H)
    total_full = total_here.reshape(n_rows, H)
    summed_full = summed.reshape(n_rows, H, HD)
    received = (
        lax.all_to_all(peak_full, "head", split_axis=1, concat_axis=1, tiled=True),
        lax.all_to_all(total_full, "head", split_axis=1, concat_axis=1, tiled=True),
        lax.all_to_all(summed_full, "head", split_axis=1, concat_axis=1, tiled=True),
    )
    peak_source = received[0].reshape(n_rows, n_head, heads_here)
    total_source = received[1].reshape(n_rows, n_head, heads_here)
    summed_source = received[2].reshape(n_rows, n_head, heads_here, HD)
    owned_group = my_index * heads_here // group_size
    key_owned = lax.dynamic_index_in_dim(fresh_keys, owned_group, 1, keepdims=False)
    fresh_score = (
        jnp.einsum("rjd,rd->rj", own_query, key_owned, preferred_element_type=jnp.float32)
        * score_scale
    )
    value_owned = lax.dynamic_index_in_dim(fresh_values, owned_group, 1, keepdims=False)
    fresh_spread = jnp.broadcast_to(value_owned[:, None, :], (n_rows, heads_here, HD))
    attended = settle(peak_source, total_source, summed_source, fresh_score, fresh_spread)
    local_table = hadamard(heads_here)
    rotated = jnp.einsum(
        "kj,rjd->rkd", local_table, attended.astype(jnp.float32), precision=lax.Precision.HIGHEST
    )
    for bit_pos in range(n_head.bit_length() - 1):
        partner = partner_2(rotated, "head", bit_pos)
        is_upper = jnp.right_shift(my_index, bit_pos) % 2 == 1
        rotated = jnp.where(is_upper, partner - rotated, rotated + partner)
    flat_rows = (rotated * H ** (-0.5)).reshape(n_rows, heads_here * HD).astype(jnp.bfloat16)
    partial_out = jnp.dot(flat_rows, wo_codes, preferred_element_type=jnp.float32)
    shares = lax.psum_scatter(partial_out, "head", scatter_dimension=1, tiled=True)
    return (residual.astype(jnp.float32) + shares * wo_scales).astype(jnp.bfloat16)


PEAK_FLOOR = -1e29
DEVICE = pl.DeviceIdType.MESH


def fused_kernel(
    n,
    positions_far,
    lengths_far,
    rates_far,
    queries_far,
    new_kv_far,
    kv_scales_far,
    kv_codes,
    wo_codes,
    out,
    positions,
    lengths,
    rates,
    queries,
    new_kv,
    kv_scales,
    in_sem,
    q_all,
    kv_here,
    scale_lanes,
    part_out,
    part_in,
    rot_out,
    rot_in,
    wo_here,
    share_out,
    share_in,
    kv_sem,
    wo_sem,
    q_send,
    q_recv,
    part_send,
    part_recv,
    rot_send,
    rot_recv,
    share_send,
    share_recv,
):
    me = lax.axis_index("head")
    core = lax.axis_index("dp")
    replica = lax.axis_index("group")
    n_rows = queries.shape[0]
    group = queries.shape[1] // HD
    block_len = kv_codes.shape[2]
    wide = wo_here.shape[2]
    half_wide = wide // 2
    halves = n_rows * block_len // HD
    rows_half = n_rows // halves
    score_scale = HD ** (-0.5)
    f32 = jnp.float32

    n_bits = n.bit_length() - 1
    bits = [lax.rem(lax.div(me, 2**b), 2) for b in range(n_bits)]
    peers = [
        sum((1 - bits[b] if step >> b & 1 else bits[b]) * 2**b for b in range(n_bits))
        for step in range(n)
    ]
    other_core = 1 - core

    def peer_of(step):
        return peers[step]

    def peer_at(step):
        peer = 0
        for b in range(n_bits):
            bit = lax.rem(lax.div(step, 2**b), 2)
            peer += (bits[b] + bit - 2 * bits[b] * bit) * 2**b
        return peer

    def side_of(other):
        return other_core if other else core

    def to(head, dp):
        return {"group": replica, "head": head, "dp": dp}

    fetched = [
        pltpu.make_async_copy(far, near, in_sem.at[k])
        for k, (far, near) in enumerate(
            [
                (positions_far, positions),
                (rates_far, rates),
                (queries_far, queries),
                (lengths_far, lengths),
                (kv_scales_far, kv_scales),
                (new_kv_far, new_kv),
            ]
        )
    ]
    for copy in fetched:
        copy.start()
    kv_copy = pltpu.make_async_copy(kv_codes, kv_here, kv_sem)
    kv_copy.start()

    def wo_copy(i):
        first = pl.multiple_of(i * (2 * wide) + core * wide, wide)
        return pltpu.make_async_copy(
            wo_codes.at[:, pl.ds(first, wide)], wo_here.at[i], wo_sem.at[i]
        )

    barrier = pltpu.get_barrier_semaphore()
    for step in range(n):
        for other in range(2):
            if step or other:
                pl.semaphore_signal(
                    barrier,
                    inc=1,
                    device_id=to(peer_of(step), side_of(other)),
                    device_id_type=DEVICE,
                )

    lane_1 = lax.broadcasted_iota(jnp.int32, (1, HD), 1)
    row_8 = lax.broadcasted_iota(jnp.int32, (n_rows, HD), 0)
    for copy in fetched[:3]:
        copy.wait()
    pos = jnp.zeros((n_rows, HD), f32)
    for r in range(n_rows):
        pos = jnp.where(row_8 == r, positions[r].astype(f32), pos)
    sign = jnp.where(lane_1 < HD // 2, -1.0, 1.0).astype(f32)
    angle = pos * rates[...]
    cosine = jnp.cos(angle)
    sine = jnp.sin(angle) * sign

    def turn(v, c, s):
        return v * c + pltpu.roll(v, HD // 2, 1) * s

    stacked = jnp.concatenate(
        [
            turn(queries[:, j * HD : (j + 1) * HD].astype(f32), cosine, sine)
            for j in range(group)
        ],
        axis=0,
    ).astype(jnp.bfloat16)

    def permutation(major, minor):
        size = major * minor
        to_row = lax.broadcasted_iota(jnp.int32, (size, size), 0)
        from_row = lax.broadcasted_iota(jnp.int32, (size, size), 1)
        shift = minor.bit_length() - 1
        wanted = (to_row & (minor - 1)) * major + (to_row >> shift)
        return jnp.where(wanted == from_row, 1.0, 0.0).astype(jnp.bfloat16)

    q_all[me] = jnp.dot(
        permutation(n_rows, group), stacked, preferred_element_type=f32
    ).astype(jnp.bfloat16)

    pl.semaphore_wait(barrier, 2 * n - 1)

    def q_copy(step):
        return pltpu.make_async_remote_copy(
            src_ref=q_all.at[me],
            dst_ref=q_all.at[me],
            send_sem=q_send.at[step],
            recv_sem=q_recv.at[me],
            device_id=to(peer_of(step), core),
            device_id_type=DEVICE,
        )

    def q_forward(step):
        block = peer_of(step)
        return pltpu.make_async_remote_copy(
            src_ref=q_all.at[block],
            dst_ref=q_all.at[block],
            send_sem=q_send.at[step + 1],
            recv_sem=q_recv.at[block],
            device_id=to(peer_of(1), core),
            device_id_type=DEVICE,
        )

    def q_arrival(source):
        return pltpu.make_async_remote_copy(
            src_ref=q_all.at[source],
            dst_ref=q_all.at[source],
            send_sem=q_send.at[0],
            recv_sem=q_recv.at[source],
            device_id=to(source, core),
            device_id_type=DEVICE,
        )

    direct = [1] + list(range(2, n, 2))
    for step in direct:
        q_copy(step).start()
    for step in (n - 1, n - 2):
        wo_copy(peer_of(step)).start()
    for copy in fetched[3:]:
        copy.wait()

    for which in range(2):
        for half in range(halves):
            scale_lanes[which, half] = jnp.concatenate(
                [
                    kv_scales[half * rows_half + r, which]
                    for r in range(rows_half)
                ],
                axis=1,
            ) * (score_scale if which == 0 else 1.0)
    shape = (rows_half * group, HD)
    row_of = lax.broadcasted_iota(jnp.int32, shape, 0) >> (group.bit_length() - 1)
    lane = lax.broadcasted_iota(jnp.int32, shape, 1)
    slot = me * block_len + (lane & (block_len - 1))
    lane_row = lane >> (block_len.bit_length() - 1)
    masks = []
    for half in range(halves):
        live = jnp.zeros(shape, jnp.int32)
        for r in range(rows_half):
            live = jnp.where(row_of == r, lengths[half * rows_half + r], live)
        masks.append(
            jnp.where(
                (row_of == lane_row) & (slot < live), 0.0, NEG_FILL
            ).astype(f32)
        )

    kv_copy.wait()

    def attend(g, stats):
        lanes = pl.ds(pl.multiple_of(g * HD, HD), HD)
        result = []
        for half in range(halves):
            first = half * rows_half
            keys = kv_here[first : first + rows_half, 0, :, lanes].reshape(HD, HD)
            values = kv_here[first : first + rows_half, 1, :, lanes].reshape(HD, HD)
            query = q_all[g, half * shape[0] : (half + 1) * shape[0], :]
            raw = lax.dot_general(
                query, keys, (((1,), (1,)), ((), ())), preferred_element_type=f32
            )
            scores = raw * scale_lanes[0, half, pl.ds(g, 1), :] + masks[half]
            peak = jnp.maximum(jnp.max(scores, axis=1, keepdims=True), PEAK_FLOOR)
            weights = jnp.exp(scores - peak)
            total = jnp.sum(weights, axis=1, keepdims=True)
            weighted = weights * scale_lanes[1, half, pl.ds(g, 1), :]
            summed = jnp.dot(
                weighted.astype(jnp.bfloat16), values, preferred_element_type=f32
            ).astype(jnp.bfloat16)
            part_out[first : first + rows_half, g + 1] = summed.reshape(
                rows_half, group, HD
            )
            stat = stats[half]
            stat = jnp.where(lane == g, peak, stat)
            result.append(jnp.where(lane == g + n, total, stat))
        return tuple(result)

    block = lax.div(me, n // 2)

    def part_copy(step, first, count):
        return pltpu.make_async_remote_copy(
            src_ref=part_out.at[peer_of(step), pl.ds(first, count)],
            dst_ref=part_in.at[me, pl.ds(first, count)],
            send_sem=part_send,
            recv_sem=part_recv,
            device_id=to(peer_of(step), core),
            device_id_type=DEVICE,
        )

    def arrivals(buffer, send, recv):
        return pltpu.make_async_remote_copy(
            src_ref=buffer.at[pl.ds(0, n - 1), pl.ds(0, n + 1)],
            dst_ref=buffer.at[pl.ds(0, n - 1), pl.ds(0, n + 1)],
            send_sem=send,
            recv_sem=recv,
            device_id=to(peer_of(1), core),
            device_id_type=DEVICE,
        )

    def send_part(last):
        if last:
            first, count = (1 - block) * (n // 2 + 1), n // 2 + 1
        else:
            first, count = block * (n // 2) + 1, n // 2
        for s in reversed(range(1, n)):
            part_copy(s, first, count).start()

    def await_q(step):
        q_arrival(peer_of(step)).wait_recv()

    stats = attend(me, tuple(jnp.zeros(shape, f32) for _ in range(halves)))
    for step in range(1, n, 2):
        if step + 1 < n:
            await_q(step + 1)
            q_forward(step + 1).start()
        await_q(step)
        stats = attend(peer_of(step), stats)
        if step + 1 < n:
            stats = attend(peer_of(step + 1), stats)
        else:
            for half in range(halves):
                for r in range(rows_half):
                    exact = stats[half][r * group : (r + 1) * group]
                    packed = jnp.zeros((group, HD), f32)
                    for piece in range(3):
                        rounded = exact.astype(jnp.bfloat16).astype(f32)
                        exact = exact - rounded
                        if piece:
                            rounded = pltpu.roll(rounded, piece * 2 * n, 1)
                        packed = packed + rounded
                    packed = packed.astype(jnp.bfloat16)
                    part_out[half * rows_half + r, 0] = packed
                    part_out[half * rows_half + r, n + 1] = packed
            send_part(True)
        if step == n // 2 - 1:
            send_part(False)
        if n - 2 - step >= 1:
            wo_copy(peer_of(n - 2 - step)).start()
        if n - 3 - step >= 0:
            wo_copy(peer_of(n - 3 - step)).start()
    part_in[me] = part_out[me]

    fresh_pair = new_kv[me].astype(f32)
    angle_me = positions[me].astype(f32) * rates[...]
    cosine_me = jnp.cos(angle_me)
    sine_me = jnp.sin(angle_me) * sign
    fresh_keys = [
        turn(
            jnp.broadcast_to(fresh_pair[0:1, g * HD : (g + 1) * HD], (8, HD)),
            cosine_me,
            sine_me,
        )[0:1].astype(jnp.bfloat16).astype(f32)
        for g in range(n)
    ]
    fresh_values = [fresh_pair[1:2, g * HD : (g + 1) * HD] for g in range(n)]

    common = lax.broadcasted_iota(jnp.int32, (H, H), 0) & lax.broadcasted_iota(
        jnp.int32, (H, H), 1
    )
    parity = jnp.zeros((H, H), jnp.int32)
    for b in range(H.bit_length() - 1):
        parity = parity ^ (lax.shift_right_logical(common, b) & 1)
    sylvester = jnp.where(parity == 0, 1.0, -1.0).astype(jnp.bfloat16)

    order = permutation(group, 2 * n_rows)
    lane_g = lax.broadcasted_iota(jnp.int32, (group, HD), 1)
    fresh = jnp.zeros((group, HD), f32)
    own_rows = pl.ds(pl.multiple_of(me * group, group), group)
    for g in range(n):
        score = jnp.sum(
            q_all[g, own_rows, :].astype(f32) * fresh_keys[g], axis=1, keepdims=True
        )
        fresh = jnp.where(lane_g == g, score * score_scale, fresh)

    arrivals(part_in, part_send, part_recv).wait_recv()
    stat = []
    for s in range(n):
        packed = part_in[s, n + 1 if s < n // 2 else 0].astype(f32)
        stat.append(
            packed
            + pltpu.roll(packed, HD - 2 * n, 1)
            + pltpu.roll(packed, HD - 4 * n, 1)
        )
    top = fresh
    for s in range(n):
        top = jnp.maximum(top, stat[s])
    factor = [jnp.exp(stat[s] - top) for s in range(n)]
    fresh_factor = jnp.exp(fresh - top)
    total = fresh_factor
    for s in range(n):
        total = total + factor[s] * pltpu.roll(stat[s], HD - n, 1)
    inverse = 1.0 / total
    factor = [f * inverse for f in factor]
    fresh_factor = fresh_factor * inverse

    attended = []
    for g in range(n):
        mixed = fresh_factor[:, g : g + 1] * fresh_values[g]
        for s in range(n):
            mixed = mixed + factor[s][:, g : g + 1] * part_in[s, g + 1].astype(f32)
        attended.append(mixed)
    attended = jnp.concatenate(attended, axis=0).astype(jnp.bfloat16)
    rotated = jnp.dot(sylvester, attended, preferred_element_type=f32) * (H ** (-0.5))
    rot_out[...] = rotated.astype(jnp.bfloat16).reshape(n, group, HD)

    def rot_copy(step, other):
        peer = peer_of(step)
        return pltpu.make_async_remote_copy(
            src_ref=rot_out.at[peer],
            dst_ref=rot_in.at[core, me],
            send_sem=rot_send.at[other],
            recv_sem=rot_recv.at[core],
            device_id=to(peer, side_of(other)),
            device_id_type=DEVICE,
        )

    def rot_arrival(other):
        side = side_of(other)
        count = pl.ds(0, n - 1 + other)
        return pltpu.make_async_remote_copy(
            src_ref=rot_out.at[count],
            dst_ref=rot_in.at[side, count],
            send_sem=rot_send.at[other],
            recv_sem=rot_recv.at[side],
            device_id=to(peer_of(1), side),
            device_id_type=DEVICE,
        )

    pairs = [(s, o) for s in reversed(range(n)) for o in range(2) if s or o]
    for step, other in pairs:
        rot_copy(step, other).start()
    rot_in[core, me] = rot_out[me]
    for other in range(2):
        rot_arrival(other).wait_recv()
    tiles = jnp.dot(
        order, rot_in[...].reshape(2 * n_rows * group, HD), preferred_element_type=f32
    ).astype(jnp.bfloat16)
    flat_rows = jnp.concatenate(
        [tiles[k * 2 * n_rows : (k + 1) * 2 * n_rows] for k in range(group)], axis=1
    )

    def share_copy(i, other):
        side = side_of(other)
        return pltpu.make_async_remote_copy(
            src_ref=share_out.at[side, i],
            dst_ref=share_in.at[core, me],
            send_sem=share_send.at[other],
            recv_sem=share_recv.at[core],
            device_id=to(i, side),
            device_id_type=DEVICE,
        )

    def share_arrival(other):
        side = side_of(other)
        count = pl.ds(0, n - 1 + other)
        return pltpu.make_async_remote_copy(
            src_ref=share_out.at[side, count],
            dst_ref=share_in.at[side, count],
            send_sem=share_send.at[other],
            recv_sem=share_recv.at[side],
            device_id=to(peer_of(1), side),
            device_id_type=DEVICE,
        )

    def project(pair):
        for i in pair:
            wo_copy(i).wait()
        shares = [
            jnp.dot(flat_rows, wo_here[i], preferred_element_type=f32) for i in pair
        ]
        for i, share in zip(pair, shares):
            for side in range(2):
                rows = share[side * n_rows : (side + 1) * n_rows]
                share_out[side, i] = jnp.concatenate(
                    [rows[:, :half_wide], rows[:, half_wide:]], axis=0
                ).astype(jnp.bfloat16)

    def project_step(step, carry):
        pair = [peer_at(n - 1 - 2 * step), peer_at(n - 2 - 2 * step)]
        project(pair)
        for i in pair:
            share_copy(i, 0).start()
            share_copy(i, 1).start()
        return carry

    lax.fori_loop(0, n // 2 - 1, project_step, 0)
    project([peers[1], me])
    share_copy(peers[1], 0).start()
    share_copy(peers[1], 1).start()
    share_copy(me, 1).start()
    share_in[core, me] = share_out[core, me]

    for other in range(2):
        share_arrival(other).wait_recv()
    for side in range(2):
        added = share_in[side, 0].astype(f32)
        for s in range(1, n):
            added = added + share_in[side, s].astype(f32)
        for half in range(2):
            first = side * wide + half * half_wide
            out[:, first : first + half_wide] = added[half * n_rows : (half + 1) * n_rows]

    for step in direct:
        q_copy(step).wait_send()
    for step in direct[1:]:
        q_forward(step).wait_send()
    arrivals(part_out, part_send, part_recv).wait_send()
    for other in range(2):
        rot_arrival(other).wait_send()
        share_arrival(other).wait_send()


def on_device_fused(
    queries, new_kv, positions, lengths, kv_codes, kv_scales, wo_codes, wo_scales, residual
):
    n = lax.axis_size("head")
    n_rows = queries.shape[0]
    group = queries.shape[1] // HD
    block_len = kv_codes.shape[2]
    width = wo_codes.shape[1]
    wide = width // n // 2
    halves = n_rows * block_len // HD
    rates = ROPE_BASE ** (-np.arange(HD // 2) * (2.0 / HD))
    rates = np.tile(rates, 2)[None, :].astype(np.float32)
    bf16, f32 = jnp.bfloat16, jnp.float32
    vmem = pl.BlockSpec(memory_space=pltpu.VMEM)
    hbm = pl.BlockSpec(memory_space=pltpu.HBM)
    dma = pltpu.SemaphoreType.DMA
    shares = pl.pallas_call(
        functools.partial(fused_kernel, n),
        out_shape=jax.ShapeDtypeStruct(residual.shape, f32),
        in_specs=[hbm] * 8,
        out_specs=vmem,
        scratch_shapes=[
            pltpu.SMEM(positions.shape, jnp.int32),
            pltpu.SMEM(lengths.shape, jnp.int32),
            pltpu.VMEM(rates.shape, f32),
            pltpu.VMEM(queries.shape, bf16),
            pltpu.VMEM(new_kv.shape, bf16),
            pltpu.VMEM(kv_scales.shape, f32),
            dma((6,)),
            pltpu.VMEM((n, n_rows * group, HD), bf16),
            pltpu.VMEM(kv_codes.shape, bf16),
            pltpu.VMEM((2, halves, KVH, HD), f32),
            pltpu.VMEM((n, n + 2, group, HD), bf16),
            pltpu.VMEM((n, n + 2, group, HD), bf16),
            pltpu.VMEM((n, group, HD), bf16),
            pltpu.VMEM((2, n, group, HD), bf16),
            pltpu.VMEM((n, wo_codes.shape[0], wide), bf16),
            pltpu.VMEM((2, n, 2 * n_rows, wide // 2), bf16),
            pltpu.VMEM((2, n, 2 * n_rows, wide // 2), bf16),
            dma,
            dma((n,)),
            dma((n + 1,)),
            dma((n,)),
            dma,
            dma,
            dma((2,)),
            dma((2,)),
            dma((2,)),
            dma((2,)),
        ],
        compiler_params=pltpu.CompilerParams(
            collective_id=0, has_side_effects=True, vmem_limit_bytes=64 * 1024 * 1024
        ),
        cost_estimate=pl.CostEstimate(
            flops=2 * 2 * n_rows * wo_codes.shape[0] * width // 2,
            bytes_accessed=wo_codes.shape[0] * width,
            transcendentals=0,
        ),
    )(
        positions,
        lengths,
        rates,
        queries,
        new_kv,
        kv_scales,
        kv_codes,
        wo_codes,
    )
    return (residual.astype(f32) + shares * wo_scales).astype(bf16)


def on_device(*arrays):
    queries, kv_codes, wo_codes = arrays[0], arrays[4], arrays[6]
    n = lax.axis_size("head")
    n_rows, group, block_len = queries.shape[0], queries.shape[1] // HD, kv_codes.shape[2]
    fits = (
        lax.axis_size("dp") == 2
        and n == KVH == n_rows
        and n & (n - 1) == 0
        and group == H // KVH == 16
        and block_len % 16 == 0
        and block_len < HD
        and HD % block_len == 0
        and n_rows * block_len % HD == 0
        and wo_codes.shape[1] % (n * 512) == 0
    )
    return (on_device_fused if fits else on_device_general)(*arrays)


def solution(mesh):
    placed = (
        P(("group", "dp"), "head"),
        P(("group", "dp"), None, None),
        P(("group", "dp")),
        P(("group", "dp")),
        P(("group", "dp"), None, "head", None),
        P(("group", "dp"), None, None, "head"),
        P("head", None),
        P("head"),
        P(("group", "dp"), "head"),
    )
    return jax.shard_map(
        on_device, mesh=mesh, in_specs=placed, out_specs=P(("group", "dp"), "head"), check_vma=False
    )
```
